32 devices in a mesh: dp: 8 (over z, x), tensor: 4 (over y, core).
Axes of the slice: x: 2, y: 2, z: 4, core: 2. Of those that a mesh axis runs over, the one named last changes fastest.
Arguments:
- hidden_in: bfloat16 [8192, 1152], P(('dp', 'tensor')), may hold values from -6 to 6
- picture_ids: int32 [8192], P('dp'), may hold values from -1 to 9, as said below
- norm1_gain: float32 [1152], replicated, may hold values from 0.5 to 1.5
- norm1_bias: float32 [1152], replicated, may hold values from -1.75 to 1.75
- w_qkv: bfloat16 [3, 1152, 1152], P(None, None, 'tensor'), may hold values from -1 to 1
- qv_bias: float32 [2, 1152], P(None, 'tensor'), may hold values from -3 to 3
- w_out: bfloat16 [1152, 1152], P('tensor'), may hold values from -0.75 to 0.75
- out_bias: float32 [1152], replicated, may hold values from -1.75 to 1.75
- norm2_gain: float32 [1152], replicated, may hold values from 0.5 to 1.5
- norm2_bias: float32 [1152], replicated, may hold values from -1.75 to 1.75
- w_up: bfloat16 [1152, 4304], P(None, 'tensor'), may hold values from -0.1875 to 0.1875
- up_bias: float32 [4304], P('tensor'), may hold values from -3 to 3
- w_down: bfloat16 [4304, 1152], P('tensor'), may hold values from -0.125 to 0.125
- down_bias: float32 [1152], replicated, may hold values from -1.75 to 1.75
- cotangent: bfloat16 [8192, 1152], P(('dp', 'tensor')), may hold values from -6 to 6
Outputs:
- hidden_out: bfloat16 [8192, 1152], P(('dp', 'tensor'))
- grad_in: bfloat16 [8192, 1152], P(('dp', 'tensor'))
- grad_qkv: float32 [3, 1152, 1152], P(None, 'dp', 'tensor')
- grad_out: float32 [1152, 1152], P('tensor', 'dp')
- grad_up: float32 [1152, 4304], P('dp', 'tensor')
- grad_down: float32 [4304, 1152], P('tensor', 'dp')
- grad_qv_bias: float32 [2, 1152], P(None, 'tensor')
- grad_up_bias: float32 [4304], P('tensor')
- grad_shared: float32 [6, 1152], replicated
- head_maxima: float32 [16], P('tensor')
- scaled_qk: bfloat16 [2, 1152, 1152], P(None, None, 'tensor')
- scaled_query_bias: float32 [1152], P('tensor')
The draws below stay inside these ranges and needn't reach their ends.
Inputs may be any that keep to these rules, and one draw needn't show every extreme that they name: `picture_ids`: each aligned row of 1024 tokens holds whole pictures of 100 to 1024 patches one after another, numbered from 0 within the row, then padding with id -1; some row holds a single picture of 1024 patches, and some other row holds 10 pictures of 100 patches.
All inputs are finite; a program needn't handle non-finite values.
Results may differ from the reference program's by a relative error of at most 0.014.
Values may be sent and summed in bfloat16 or wider, within the bound.
No kernel may reach another device: no remote copies, remote signals or barrier semaphores. Data moves between devices by JAX's collectives and lax.ppermute only.
A program may use at most 192 MiB of HBM per device.

```python
import math
import jax
import jax.numpy as jnp
from jax import lax

D = 1152
HEADS = 16
HEAD_DIM = 72
FF = 4304
PACK = 1024
PIC_MIN = 100
CLIP_LIMIT = 9
ROWS = 8
TOKENS = 8192


def draw_picture_ids(key, part):
    key = jax.random.fold_in(key, 7)
    row_count = TOKENS // PACK
    most_pics = PACK // PIC_MIN + 1
    key_len, key_row, key_other = jax.random.split(key, 3)
    lengths = jax.random.randint(key_len, (row_count, most_pics), PIC_MIN, PACK + 1)
    full_row = jax.random.randint(key_row, (), 0, row_count)
    small_row = (full_row + jax.random.randint(key_other, (), 1, row_count)) % row_count
    row_index = jnp.arange(row_count, dtype=jnp.int32)
    lengths = jnp.where(row_index[:, None] == small_row, PIC_MIN, lengths)
    lengths = lengths.at[full_row, 0].set(PACK)
    ends_at = jnp.cumsum(lengths, axis=1)
    fits = ends_at <= PACK
    live_end = jnp.max(jnp.where(fits, ends_at, 0), axis=1)
    places = jnp.arange(PACK, dtype=jnp.int32)
    index_in = jnp.sum((ends_at[:, None, :] <= places[None, :, None]).astype(jnp.int32), axis=2)
    picture = jnp.where(places[None, :] < live_end[:, None], index_in, -1)
    return picture.reshape(TOKENS).astype(jnp.int32)


def draw_w_qkv(key, part):
    key = jax.random.fold_in(key, 11)
    key_base, key_order = jax.random.split(key)
    base = jax.random.truncated_normal(key_base, -3.0, 3.0, (3, D, D), jnp.float32)
    order = jax.random.permutation(key_order, HEADS).astype(jnp.float32)
    low_end = jnp.log(jnp.float32(0.67))
    high_end = jnp.log(jnp.float32(1.14))
    head_scale = jnp.exp(low_end + (high_end - low_end) * order / max(HEADS - 1, 1))
    column_scale = jnp.repeat(head_scale, HEAD_DIM)
    unit_scale = jnp.ones((D,), jnp.float32)
    per_matrix = jnp.stack([column_scale, column_scale, unit_scale])
    return (base * per_matrix[:, None, :] * (D // 2) ** (-0.5)).astype(jnp.bfloat16)


def with_spikes(entries, rng, source, target, shards_of, factor):
    owner, partner = [(jnp.arange(entries.shape[position]) // (entries.shape[position] // shards_of)).reshape([-1 if axis == position else 1 for axis in range(entries.ndim)]) for position in (source, target)]
    chosen = jax.random.permutation(rng, shards_of)[partner]
    strong = (owner == chosen) | (owner == (partner + shards_of // 2) % shards_of)
    return jnp.where(strong, factor * entries, entries)


def steps_of(rng, dims, shards, smallest, high):
    level = 1.0
    for dim, blocks in shards:
        steps = jax.random.uniform(jax.random.fold_in(jax.random.fold_in(rng, 6), dim), (blocks,), jnp.float32, smallest / len(shards), high / len(shards))
        level = level * jnp.repeat(jnp.exp(steps), dims[dim] // blocks).reshape((-1,) + (1,) * (len(dims) - 1 - dim))
    return level


def scatter_about(key, extent, spread, most, cuts=(), kind=jnp.bfloat16):
    values = spread * jax.random.normal(key, extent, jnp.float32)
    if cuts:
        values = values * steps_of(key, extent, cuts, -0.22, 0.18)
    return jnp.clip(values, -most, most).astype(kind)


def noise_with(key, shape, scale, most, shards, heavy, held_as=jnp.bfloat16):
    values = scale * jax.random.normal(key, shape, jnp.float32)
    if shards:
        values = values * steps_of(key, shape, shards, -0.22, 0.18)
    return jnp.clip(with_spikes(values, jax.random.fold_in(key, 3), *heavy), -most, most).astype(held_as)


def setup_inputs(seed: int = 0) -> dict:
    splits = jax.random.split(jax.random.key(seed), 16)
    return {
        "hidden_in": noise_with(splits[0], (TOKENS, D), 1.0, 6.0, ((0, 32),), (0, 1, 32, 2.75)),
        "picture_ids": draw_picture_ids(jax.random.fold_in(splits[15], 71), 0),
        "norm1_gain": jnp.clip(1.0 + 0.1 * jax.random.normal(splits[2], (D,), jnp.float32), 0.5, 1.5),
        "norm1_bias": scatter_about(splits[3], (D,), 0.3, 1.75, (), jnp.float32),
        "w_qkv": draw_w_qkv(jax.random.fold_in(splits[15], 71), 0),
        "qv_bias": scatter_about(splits[5], (2, D), 0.5, 3.0, ((1, 4),), jnp.float32),
        "w_out": scatter_about(splits[6], (D, D), (D // 16) ** -0.5, 0.75, ((0, 4),)),
        "out_bias": scatter_about(splits[7], (D,), 0.3, 1.75, (), jnp.float32),
        "norm2_gain": jnp.clip(1.0 + 0.1 * jax.random.normal(splits[8], (D,), jnp.float32), 0.5, 1.5),
        "norm2_bias": scatter_about(splits[9], (D,), 0.3, 1.75, (), jnp.float32),
        "w_up": scatter_about(splits[10], (D, FF), D ** -0.5, 0.1875, ((1, 4),)),
        "up_bias": scatter_about(splits[11], (FF,), 0.5, 3.0, ((0, 4),), jnp.float32),
        "w_down": scatter_about(splits[12], (FF, D), (FF // 2) ** -0.5, 0.125, ((0, 4),)),
        "down_bias": scatter_about(splits[13], (D,), 0.3, 1.75, (), jnp.float32),
        "cotangent": noise_with(splits[14], (TOKENS, D), 1.0, 6.0, ((0, 32),), (0, 1, 32, 2.75)),
    }


highest = lax.Precision.HIGHEST
eps_norm = 1e-06
neg_fill = -1e+30

@jax.custom_vjp
def low(v):
    return lax.optimization_barrier(v.astype(jnp.bfloat16)).astype(jnp.float32)

@jax.custom_vjp
def low_back(v):
    return v

def low_keep(v):
    return (low(v), None)

def low_pass(kept, grad):
    return (grad,)

def back_keep(v):
    return (v, None)

def back_low(kept, grad):
    return (low(grad),)
low.defvjp(low_keep, low_pass)
low_back.defvjp(back_keep, back_low)

def layer_norm(values_in, gain, shift):
    row_mean = lax.optimization_barrier(jnp.mean(values_in, axis=-1, keepdims=True))
    centred = values_in - row_mean
    variance = lax.optimization_barrier(jnp.mean(centred * centred, axis=-1, keepdims=True))
    return centred * lax.rsqrt(variance + eps_norm) * gain + shift

def row_attention(parts_in):
    queries, key_rows, values, picture = parts_in
    scores = jnp.einsum('qhd,khd->hqk', queries, key_rows, precision=highest) * HEAD_DIM ** (-0.5)
    scores = low_back(scores)
    allowed = picture[:, None] == picture[None, :]
    scores = jnp.where(allowed[None], scores, neg_fill)
    row_top = lax.optimization_barrier(jnp.max(scores, axis=2, keepdims=True))
    weights = jnp.exp(scores - row_top)
    prob_rows = weights / lax.optimization_barrier(jnp.sum(weights, axis=2, keepdims=True))
    attended = jnp.einsum('hqk,khd->qhd', low(prob_rows), values, precision=highest)
    return (attended, lax.optimization_barrier(jnp.max(scores, axis=(1, 2))))

def forward(hidden, gain_a, shift_a, w_qkv, qv_bias, w_out, out_bias, gain_b, shift_b, w_up, up_bias, w_down, down_bias, picture):
    row_count = hidden.shape[0] // PACK
    normed_a = low(layer_norm(hidden, gain_a, shift_a))
    projected = jnp.einsum('td,cde->cte', normed_a, w_qkv, precision=highest)
    queries = low(low_back(projected[0] + qv_bias[0]))
    key_rows = low(low_back(projected[1]))
    values = low(low_back(projected[2] + qv_bias[1]))
    head_shape = (row_count, PACK, HEADS, HEAD_DIM)
    attended, maxima = lax.map(jax.checkpoint(row_attention), (queries.reshape(head_shape), key_rows.reshape(head_shape), values.reshape(head_shape), picture.reshape(row_count, PACK)))
    attended = low(low_back(attended.reshape(row_count * PACK, D)))
    branch_a = low_back(jnp.dot(attended, w_out, precision=highest))
    residual = hidden + branch_a + out_bias
    normed_b = low(layer_norm(residual, gain_b, shift_b))
    pre_act = low_back(jnp.dot(normed_b, w_up, precision=highest) + up_bias)
    activated = low(jax.nn.gelu(pre_act, approximate=True))
    branch_b = low_back(jnp.dot(activated, w_down, precision=highest))
    return (residual + branch_b + down_bias, lax.optimization_barrier(jnp.max(maxima, axis=0)))

def reference(hidden_in, picture_ids, norm1_gain, norm1_bias, w_qkv, qv_bias, w_out, out_bias, norm2_gain, norm2_bias, w_up, up_bias, w_down, down_bias, cotangent):
    params = tuple((element.astype(jnp.float32) for element in (norm1_gain, norm1_bias, w_qkv, qv_bias, w_out, out_bias, norm2_gain, norm2_bias, w_up, up_bias, w_down, down_bias)))
    per_step = math.gcd(ROWS, 4)
    step_count = ROWS // per_step
    step_tokens = per_step * PACK

    def one_step(state_in, inputs):
        grad_sums, top_seen = state_in
        hidden, picture, grad_top = inputs

        def layer_at(hidden_f, *weights):
            return forward(hidden_f, *weights, picture)
        result, pullback, maxima = jax.vjp(layer_at, hidden.astype(jnp.float32), *params, has_aux=True)
        grad_list = pullback(grad_top.astype(jnp.float32))
        grad_sums = tuple((running + element for running, element in zip(grad_sums, grad_list[1:])))
        return ((grad_sums, jnp.maximum(top_seen, maxima)), (result.astype(jnp.bfloat16), grad_list[0].astype(jnp.bfloat16)))
    start_sums = tuple((jnp.zeros(element.shape, jnp.float32) for element in params))
    start_top = jnp.full((HEADS,), -1e+30, jnp.float32)
    (grad_sums, maxima), (out_rows, grad_rows) = lax.scan(one_step, (start_sums, start_top), (hidden_in.reshape(step_count, step_tokens, D), picture_ids.reshape(step_count, step_tokens), cotangent.reshape(step_count, step_tokens, D)))
    hidden_out = out_rows.reshape(TOKENS, D)
    grad_in = grad_rows.reshape(TOKENS, D)
    grad_shared = jnp.stack([grad_sums[0], grad_sums[1], grad_sums[5], grad_sums[6], grad_sums[7], grad_sums[11]])
    limit = jnp.float32(CLIP_LIMIT)
    factor = jnp.sqrt(limit / jnp.maximum(maxima, limit))
    column = jnp.repeat(factor, HEAD_DIM)
    scaled_qk = (w_qkv[:2].astype(jnp.float32) * column).astype(jnp.bfloat16)
    scaled_query_bias = qv_bias[0] * column
    return (hidden_out, grad_in, grad_sums[2], grad_sums[4], grad_sums[8], grad_sums[10], grad_sums[3], grad_sums[9], grad_shared, maxima, scaled_qk, scaled_query_bias)
```

```python
import jax
import jax.numpy as jnp
from jax import lax
from jax.sharding import PartitionSpec as P

HEAD_DIM = 72
PACK = 1024
CLIP_LIMIT = 9

eps_norm = 1e-06
neg_fill = -1e30
f32 = jnp.float32
bf16 = jnp.bfloat16


def swap(value, axis, size, bit):
    return lax.ppermute(value, axis, [(i, i ^ bit) for i in range(size)])


def after(value, *others):
    return lax.optimization_barrier((value,) + others)[0]


def normalize(values_in, gain, shift):
    row_mean = jnp.mean(values_in, axis=-1, keepdims=True)
    centred = values_in - row_mean
    variance = jnp.mean(centred * centred, axis=-1, keepdims=True)
    inverse = lax.rsqrt(variance + eps_norm)
    unit_rows = centred * inverse
    return (unit_rows * gain + shift, unit_rows, inverse)


def norm_back(grad_rows, unit_rows, inverse, gain):
    scaled = grad_rows * gain
    return inverse * (
        scaled
        - jnp.mean(scaled, axis=-1, keepdims=True)
        - unit_rows * jnp.mean(scaled * unit_rows, axis=-1, keepdims=True)
    )


def gelu_tanh(inputs):
    return jax.nn.gelu(inputs, approximate=True)


def dot(left, right, spec):
    return jnp.einsum(spec, left, right, preferred_element_type=f32)


def make_local(dp_size, tensor_size):
    def gather(own):
        sib = swap(own, "tensor", tensor_size, 1)
        partner = swap(own, "tensor", tensor_size, 2)
        diagonal = swap(partner, "tensor", tensor_size, 1)
        return [own, sib, partner, diagonal]

    def scatter(near, far):
        own, partner = near
        sib, diagonal = far
        got = swap(jnp.concatenate([sib, diagonal]).astype(bf16), "tensor", tensor_size, 1)
        rows = own.shape[0]
        send = (partner + got[rows:].astype(f32)).astype(bf16)
        keep = own + got[:rows].astype(f32)
        return keep + swap(send, "tensor", tensor_size, 2).astype(f32)

    def scatter_rows(value):
        index = lax.axis_index("dp")
        rows, width = value.shape
        bit = 1
        while bit < dp_size:
            left = value.shape[0] // (rows // dp_size) // 2
            block = value.reshape(left, 2, rows // dp_size, width)
            mine = (index // bit) % 2
            keep = lax.dynamic_index_in_dim(block, mine, 1, keepdims=False)
            send = lax.dynamic_index_in_dim(block, 1 - mine, 1, keepdims=False)
            got = swap(send, "dp", dp_size, bit)
            bit *= 2
            value = keep.astype(f32) + got.astype(f32)
            if bit < dp_size:
                value = value.astype(bf16)
            value = value.reshape(left * (rows // dp_size), width)
        return value

    def sum_over(value, axis, size):
        bit = 1
        while bit < size:
            value = value + swap(value, axis, size, bit)
            bit *= 2
        return value

    def local(hidden_in, picture_ids, norm1_gain, norm1_bias, w_qkv, qv_bias, w_out, out_bias,
              norm2_gain, norm2_bias, w_up, up_bias, w_down, down_bias, cotangent):
        rows = hidden_in.shape[0]
        group_rows = picture_ids.shape[0]
        head_width = w_qkv.shape[2]
        heads = head_width // HEAD_DIM
        width = hidden_in.shape[1]
        hidden_units = w_up.shape[1]
        score_scale = HEAD_DIM ** (-0.5)
        place = lax.axis_index("tensor")
        ids = jnp.concatenate([lax.dynamic_slice_in_dim(picture_ids, (place ^ k) * rows, rows) for k in range(tensor_size)])

        hidden_slots = gather(hidden_in)
        cot_slots = gather(after(cotangent, hidden_slots[3]))
        w_out_slots = gather(after(w_out, hidden_slots[3]))

        norm_slots = [normalize(part.astype(f32), norm1_gain, norm1_bias) for part in hidden_slots]
        whole_a = jnp.concatenate([part[0].astype(bf16) for part in norm_slots])
        unit_a, inverse_a = norm_slots[0][1:]
        projected = dot(whole_a, w_qkv, "td,cde->cte")
        queries = (projected[0] + qv_bias[0]).astype(bf16)
        key_rows = projected[1].astype(bf16)
        values = (projected[2] + qv_bias[1]).astype(bf16)
        query_heads = queries.reshape(group_rows, heads, HEAD_DIM)
        key_heads = key_rows.reshape(group_rows, heads, HEAD_DIM)
        value_heads = values.reshape(group_rows, heads, HEAD_DIM)

        def attend(block_q, query_ids):
            scores = dot(block_q, key_heads, "qhd,khd->hqk") * score_scale
            scores = jnp.where((query_ids[:, None] == ids[None, :])[None], scores, neg_fill)
            row_top = jnp.max(scores, axis=2, keepdims=True)
            weights = jnp.exp(scores - row_top)
            row_sum = jnp.sum(weights, axis=2, keepdims=True)
            prob_rows = (weights / row_sum).astype(bf16)
            attended = dot(prob_rows, value_heads, "hqk,khd->qhd").astype(bf16)
            return (attended.reshape(block_q.shape[0], head_width), (row_top + jnp.log(row_sum))[:, :, 0],
                    jnp.max(row_top[:, :, 0], axis=1))

        half = 2 * rows
        att_far, lse_far, top_far = attend(query_heads[half:], ids[half:])
        att_partner = swap(att_far[:rows], "tensor", tensor_size, 2)
        att_diagonal = swap(att_far[rows:], "tensor", tensor_size, 3)
        att_near, lse_near, top_near = attend(query_heads[:half], ids[:half])
        att_sib = swap(att_near[rows:], "tensor", tensor_size, 1)
        flat_att = jnp.concatenate([att_near, att_far])
        log_total = jnp.concatenate([lse_near, lse_far], axis=1)
        own_att = jnp.concatenate([att_near[:rows], att_sib, att_partner, att_diagonal], axis=1)
        whole_out = jnp.concatenate(w_out_slots)
        branch_a = dot(own_att, whole_out, "te,ed->td")
        residual = hidden_in.astype(f32) + branch_a + out_bias
        normed_b, unit_b, inverse_b = normalize(residual, norm2_gain, norm2_bias)
        whole_b = jnp.concatenate(gather(normed_b.astype(bf16)))
        whole_cot = jnp.concatenate(cot_slots)
        grad_act = dot(whole_cot, w_down, "td,fd->tf")
        pre_act = dot(whole_b, w_up, "td,df->tf") + up_bias
        activated = gelu_tanh(pre_act).astype(bf16)
        grad_pre = jax.vjp(gelu_tanh, pre_act)[1](grad_act)[0].astype(bf16)
        grad_norm_b_all = dot(grad_pre, w_up, "tf,df->td").reshape(4, rows, width)
        grad_norm_b = scatter((grad_norm_b_all[0], grad_norm_b_all[2]), (grad_norm_b_all[1], grad_norm_b_all[3]))

        grad_down = dot(whole_cot, activated, "td,tf->df").astype(bf16)
        grad_up = dot(whole_b, grad_pre, "td,tf->df").astype(bf16)
        grad_mlp = scatter_rows(jnp.concatenate([grad_up, grad_down], axis=1))
        grad_up_bias = jnp.sum(grad_pre, axis=0, dtype=f32)

        grad_top = cotangent.astype(f32)
        grad_resid = grad_top + norm_back(grad_norm_b, unit_b, inverse_b, norm2_gain)
        grad_branch = grad_resid.astype(bf16)
        grad_att_parts = dot(grad_branch, whole_out, "td,ed->te").astype(bf16)
        grad_att_slots = [grad_att_parts[:, :head_width]] + [
            swap(grad_att_parts[:, k * head_width:(k + 1) * head_width], "tensor", tensor_size, k) for k in (1, 2, 3)]
        grad_att = jnp.concatenate(grad_att_slots)
        branch_slots = gather(after(grad_branch, grad_att))
        whole_branch = jnp.concatenate(branch_slots)
        grad_out = dot(whole_branch, flat_att, "td,te->de").astype(bf16)

        branch_b_all = dot(activated, w_down, "tf,fd->td").reshape(4, rows, width)
        branch_b = scatter((branch_b_all[0], branch_b_all[2]), (branch_b_all[1], branch_b_all[3]))
        hidden_out = (residual + branch_b + down_bias).astype(bf16)

        grad_heads = grad_att.reshape(group_rows, heads, HEAD_DIM)
        scores = dot(query_heads, key_heads, "qhd,khd->hqk") * score_scale
        scores = jnp.where((ids[:, None] == ids[None, :])[None], scores, neg_fill)
        prob_full = jnp.exp(scores - log_total[:, :, None])
        grad_probs = dot(grad_heads, value_heads, "qhd,khd->hqk")
        inner = jnp.sum(prob_full * grad_probs, axis=2, keepdims=True)
        grad_scores = (prob_full * (grad_probs - inner)).astype(bf16)
        query_grad = dot(grad_scores, key_heads, "hqk,khd->qhd") * score_scale
        key_grad = dot(grad_scores, query_heads, "hqk,qhd->khd") * score_scale
        value_grad = dot(prob_full.astype(bf16), grad_heads, "hqk,qhd->khd")
        grad_stack = jnp.concatenate([query_grad.astype(bf16).reshape(group_rows, head_width),
                                      key_grad.astype(bf16).reshape(group_rows, head_width),
                                      value_grad.astype(bf16).reshape(group_rows, head_width)], axis=1)
        flat_w = jnp.concatenate([w_qkv[0], w_qkv[1], w_qkv[2]], axis=1)
        grad_norm_a_all = dot(grad_stack, flat_w, "te,de->td").reshape(4, rows, width)
        grad_norm_a = scatter((grad_norm_a_all[0], grad_norm_a_all[2]), (grad_norm_a_all[1], grad_norm_a_all[3]))
        grad_qkv = dot(whole_a, grad_stack, "td,te->de").astype(bf16)
        grad_att_w = scatter_rows(jnp.concatenate([grad_qkv, grad_out], axis=1))
        grad_in = (grad_resid + norm_back(grad_norm_a, unit_a, inverse_a, norm1_gain)).astype(bf16)

        top = jnp.maximum(top_far, top_near)
        bit = 1
        while bit < dp_size:
            top = jnp.maximum(top, swap(top, "dp", dp_size, bit))
            bit *= 2
        limit = jnp.float32(CLIP_LIMIT)
        factor = jnp.sqrt(limit / jnp.maximum(top, limit))
        column = jnp.repeat(factor, HEAD_DIM)
        scaled_qk = (w_qkv[:2].astype(f32) * column).astype(bf16)
        scaled_query_bias = qv_bias[0] * column

        small = jnp.concatenate([jnp.sum(grad_stack[:, :head_width], axis=0, dtype=f32),
                                 jnp.sum(grad_stack[:, 2 * head_width:], axis=0, dtype=f32), grad_up_bias])
        shared_part = jnp.concatenate([
            jnp.sum(grad_norm_a * unit_a, axis=0), jnp.sum(grad_norm_a, axis=0), jnp.sum(grad_resid, axis=0),
            jnp.sum(grad_norm_b * unit_b, axis=0), jnp.sum(grad_norm_b, axis=0), jnp.sum(grad_top, axis=0)])
        summed = sum_over(jnp.concatenate([small, shared_part]), "dp", dp_size)
        count = small.shape[0]
        grad_qv_bias = summed[:2 * head_width].reshape(2, head_width)
        grad_up_bias = summed[2 * head_width:count]
        grad_shared = sum_over(summed[count:], "tensor", tensor_size).reshape(6, width)
        g_up = grad_mlp[:, :hidden_units]
        g_down = grad_mlp[:, hidden_units:].T
        g_qkv = grad_att_w[:, :3 * head_width].reshape(-1, 3, head_width).transpose(1, 0, 2)
        g_out = grad_att_w[:, 3 * head_width:].T
        return (hidden_out, grad_in, g_qkv, g_out, g_up, g_down, grad_qv_bias, grad_up_bias, grad_shared,
                top, scaled_qk, scaled_query_bias)

    return local


def solution(mesh):
    return jax.shard_map(
        make_local(mesh.shape["dp"], mesh.shape["tensor"]),
        mesh=mesh,
        in_specs=(
            P(("dp", "tensor"), None), P("dp"), P(), P(), P(None, None, "tensor"), P(None, "tensor"),
            P("tensor", None), P(), P(), P(), P(None, "tensor"), P("tensor"), P("tensor", None), P(),
            P(("dp", "tensor"), None),
        ),
        out_specs=(
            P(("dp", "tensor"), None), P(("dp", "tensor"), None), P(None, "dp", "tensor"), P("tensor", "dp"),
            P("dp", "tensor"), P("tensor", "dp"), P(None, "tensor"), P("tensor"), P(), P("tensor"),
            P(None, None, "tensor"), P("tensor"),
        ),
        check_vma=False,
    )
```

```python
import functools
import math

import jax
import jax.numpy as jnp
from jax import lax
from jax.experimental import pallas as pl
from jax.experimental.pallas import tpu as pltpu
from jax.sharding import PartitionSpec as P

HEAD_DIM = 72
PACK = 1024
CLIP_LIMIT = 9
LANES = 128
SPARE = LANES - HEAD_DIM
SCALE = HEAD_DIM ** (-0.5)
LOG2E = 1.4426950408889634
GELU_A = 0.7978845608028654
GELU_B = 0.044715

eps_norm = 1e-06
neg_fill = -1e30
f32 = jnp.float32
bf16 = jnp.bfloat16
NN = (((1,), (0,)), ((), ()))
NT = (((1,), (1,)), ((), ()))
TN = (((0,), (0,)), ((), ()))


def mm(left, right, dims=NN):
    return lax.dot_general(left, right, dims, preferred_element_type=f32)


def swap(value, axis, size, bit):
    return lax.ppermute(value, axis, [(i, i ^ bit) for i in range(size)])


def after(value, *others):
    return lax.optimization_barrier((value,) + others)[0]


class Far:
    def __init__(self, value):
        self.value = value


class Lazy:
    def __init__(self, ref, copy):
        self.ref, self.copy, self.shape, self.dtype = ref, copy, ref.shape, ref.dtype

    def __getitem__(self, index):
        if self.copy is not None:
            self.copy.wait()
            self.copy = None
        return self.ref[index]


class Out:
    def __init__(self, ref, copy):
        self.ref, self.copy, self.shape, self.dtype, self.left = ref, copy, ref.shape, ref.dtype, False

    def __getitem__(self, index):
        return self.ref[index]

    def __setitem__(self, index, value):
        self.ref[index] = value

    def leave(self):
        if not self.left:
            self.copy.start()
            self.left = True


def leave(ref):
    if isinstance(ref, Out):
        ref.leave()


class Order:
    def __init__(self):
        self.last = None


def call(order, kernel, outs, ins, name, flops, scratch=(), limit=9, smem=0, waits=()):
    near = pl.BlockSpec(memory_space=pltpu.VMEM)
    far = pl.BlockSpec(memory_space=pltpu.HBM)
    scalar = pl.BlockSpec(memory_space=pltpu.SMEM)
    in_far = [isinstance(x, Far) for x in ins]
    out_far = [isinstance(x, Far) for x in outs]
    ins = [x.value if isinstance(x, Far) else x for x in ins]
    outs = [x.value if isinstance(x, Far) else x for x in outs]
    moved = sum(x.size * x.dtype.itemsize for x in outs + ins)
    unread = ([] if order.last is None else [order.last]) + list(waits)
    count, extra = len(ins), len(scratch)
    buffers = [pltpu.VMEM(x.shape, x.dtype) for x, f in zip(ins + outs, in_far + out_far) if f]

    def body(*refs):
        in_refs, refs = refs[:count], refs[count + len(unread):]
        out_refs, refs = refs[:len(outs)], refs[len(outs) + 1:]
        own, refs = refs[:extra], refs[extra:]
        buffer_refs, sems = list(refs[:len(buffers)]), refs[len(buffers):]
        slot = 0
        given, leaving = [], []
        for ref, f in zip(in_refs, in_far):
            if f:
                copy = pltpu.make_async_copy(ref, buffer_refs[slot], sems[0].at[slot])
                copy.start()
                ref = Lazy(buffer_refs[slot], copy)
                slot += 1
            given.append(ref)
        for ref, f in zip(out_refs, out_far):
            if f:
                ref = Out(buffer_refs[slot], pltpu.make_async_copy(buffer_refs[slot], ref, sems[0].at[slot]))
                leaving.append(ref)
                slot += 1
            given.append(ref)
        kernel(*given, *own)
        for ref in given:
            if isinstance(ref, Lazy) and ref.copy is not None:
                ref.copy.wait()
        for ref in leaving:
            ref.leave()
        for ref in leaving:
            ref.copy.wait()

    size = sum(math.prod(x.shape) * x.dtype.itemsize for x, f in zip(ins + outs, in_far + out_far) if f)
    results = pl.pallas_call(
        body,
        out_shape=tuple(pltpu.HBM(x.shape, x.dtype) if f else x for x, f in zip(outs, out_far))
        + (pltpu.HBM((8, LANES), f32),),
        in_specs=[scalar] * smem + [far if f else near for f in in_far[smem:]] + [pl.BlockSpec(memory_space=pl.ANY)] * len(unread),
        out_specs=tuple(far if f else near for f in out_far) + (far,),
        scratch_shapes=list(scratch) + buffers + ([pltpu.SemaphoreType.DMA((len(buffers),))] if buffers else []),
        compiler_params=pltpu.CompilerParams(vmem_limit_bytes=limit * 2**20 + size + size // 4),
        cost_estimate=pl.CostEstimate(flops=int(flops), bytes_accessed=int(moved), transcendentals=0),
        name=name,
    )(*(pltpu.with_memory_space_constraint(x, pltpu.HBM) if f else x for x, f in zip(ins, in_far)), *(pltpu.with_memory_space_constraint(x, pltpu.HBM) if i == 0 and order.last is not None else x
                                                                              for i, x in enumerate(unread)))
    order.last = results[-1]
    return results[:-1]


def shape(dims, dtype):
    return jax.ShapeDtypeStruct(tuple(dims), dtype)


def row(vector):
    return vector.reshape(1, -1)


def unit_of(values_in):
    row_mean = jnp.mean(values_in, axis=-1, keepdims=True)
    centred = values_in - row_mean
    variance = jnp.mean(centred * centred, axis=-1, keepdims=True)
    inverse = lax.rsqrt(variance + eps_norm)
    return centred * inverse, inverse


def norm_back(grad_rows, unit_rows, inverse, gain):
    scaled = grad_rows * gain
    return inverse * (
        scaled
        - jnp.mean(scaled, axis=-1, keepdims=True)
        - unit_rows * jnp.mean(scaled * unit_rows, axis=-1, keepdims=True)
    )


GAIN1, SHIFT1, GAIN2, SHIFT2, OUT_BIAS, UP_BIAS, QKV_BIAS = range(7)


def qkv_kernel(vec, xa, xb, w, n_ref, p_ref, copy_ref):
    rows = xa.shape[0]
    cols = w.shape[0]
    for i, x in enumerate((xa, xb)):
        unit, _ = unit_of(x[...].astype(f32))
        n_ref[i * rows:(i + 1) * rows, :] = (
            unit * vec[GAIN1:GAIN1 + 1, :] + vec[SHIFT1:SHIFT1 + 1, :]).astype(bf16)
    leave(n_ref)
    p_ref[...] = (mm(n_ref[...], w[...], NT) + vec[QKV_BIAS:QKV_BIAS + 1, :cols]).astype(bf16)
    copy_ref[...] = p_ref[...]


def qkv(order, xa, xb, vec, w, **more):
    rows, width = xa.shape
    cols = w.shape[0]
    return call(
        order, qkv_kernel,
        [Far(shape((2 * rows, width), bf16)), shape((2 * rows, cols), bf16), Far(shape((2 * rows, cols), bf16))],
        [Far(vec), xa, xb, w], "qkv", 4 * rows * width * cols, **more)


def marks_kernel(place_ref, ids_ref, q_ref, k_ref):
    rows = ids_ref.shape[1]
    lane = lax.broadcasted_iota(jnp.int32, (LANES, rows), 0)
    for slot in range(ids_ref.shape[0]):
        ids = ids_ref[pl.ds(place_ref[0] ^ slot, 1), :]
        same = jnp.where((ids + 1) == lane, 1.0, 0.0).T[:, :SPARE]
        r = slice(slot * rows, (slot + 1) * rows)
        q_ref[r, :] = same.astype(bf16)
        k_ref[r, :] = jnp.where(same > 0.5, 0.0, neg_fill).astype(bf16)


def marks(order, place, ids):
    return call(order, marks_kernel, [Far(shape((ids.size, SPARE), bf16))] * 2, [place, ids], "marks", ids.size, smem=1)


def attend_kernel(p_ref, kn, kf, mark_q, mark_k, oa_ref, ob_ref, lse_ref, top_ref, *, block, first):
    rows = p_ref.shape[0]
    cols = oa_ref.shape[1]
    heads = cols // HEAD_DIM
    factor = SCALE * LOG2E
    keys = jnp.concatenate([kn[:, cols:], kf[:, cols:]], axis=0)
    marked = mark_k[...]
    ones = jnp.where(lax.broadcasted_iota(jnp.int32, marked.shape, 1) == 0, 1.0, 0.0).astype(bf16)
    parts = [slice(h * HEAD_DIM, (h + 1) * HEAD_DIM) for h in range(heads)]
    ka = [jnp.concatenate([keys[:, p], marked], axis=1) for p in parts]
    va = [jnp.concatenate([keys[:, cols + p.start:cols + p.stop], ones], axis=1) for p in parts]
    qa = [jnp.concatenate([p_ref[:, p], mark_q[first:first + rows, :]], axis=1) for p in parts]
    blocks = rows // block
    steps = [(h, b) for h in range(heads) for b in range(blocks)]

    def score(i):
        h, b = steps[i]
        return mm(qa[h][b * block:(b + 1) * block], ka[h], NT)

    outs, lses, tops = {}, {}, {}
    ahead = score(0)
    for i, (h, b) in enumerate(steps):
        scores = ahead
        if i + 1 < len(steps):
            ahead = score(i + 1)
        top = jnp.max(scores, axis=1, keepdims=True)
        probs = jnp.exp2(scores * factor - top * factor).astype(bf16)
        out = mm(probs, va[h])
        total = out[:, HEAD_DIM:HEAD_DIM + 1]
        outs[h, b] = out[:, :HEAD_DIM] * (1.0 / total)
        lses[h, b] = top * SCALE + jnp.log(total)
        tops.setdefault(h, []).append(jnp.max(top, axis=0, keepdims=True))
    flat = [jnp.concatenate([outs[h, b] for h in range(heads)], axis=1).astype(bf16) for b in range(blocks)]
    half = blocks // 2
    oa_ref[...] = jnp.concatenate(flat[:half], axis=0)
    ob_ref[...] = jnp.concatenate(flat[half:], axis=0)
    for b in range(blocks):
        lse_ref[b * block:(b + 1) * block, :] = jnp.concatenate([lses[h, b] for h in range(heads)], axis=1)
    top_ref[...] = jnp.concatenate([functools.reduce(jnp.maximum, tops[h]) * SCALE for h in range(heads)], axis=1)


def attend(order, p, pn, pf, mark_q, mark_k, first, **more):
    rows = p.shape[0]
    cols = p.shape[1] // 3
    count = mark_k.shape[0]
    heads = cols // HEAD_DIM
    return call(
        order, functools.partial(attend_kernel, block=rows // 2, first=first),
        [Far(x) for x in [shape((rows // 2, cols), bf16)] * 2 + [shape((rows, heads), f32), shape((1, heads), f32)]],
        [p, pn, pf, Far(mark_q), Far(mark_k)], "attend", 8 * rows * count * cols, **more)


def split3(value):
    high = value.astype(bf16)
    rest = value - high.astype(f32)
    middle = rest.astype(bf16)
    return [high, middle, (rest - middle.astype(f32)).astype(bf16)]


def attend_back_kernel(*refs, block):
    (pn, pf, d0, d1, d2, d3, a0, a1, a2, a3, ln, lf, mq_ref, mk_ref,
     gn_ref, gf_ref, sum_ref, qt_ref) = refs
    rows = pn.shape[0]
    cols = d0.shape[1]
    count = 2 * rows
    heads = cols // HEAD_DIM
    factor = SCALE * LOG2E
    cat = lambda *xs: jnp.concatenate([x[...] for x in xs], axis=0)
    whole = cat(pn, pf)
    queries, keys, values = whole[:, :cols], whole[:, cols:2 * cols], whole[:, 2 * cols:]
    grads, outs, lse = cat(d0, d1, d2, d3), cat(a0, a1, a2, a3), cat(ln, lf)
    mark_q, mark_k = mq_ref[:, :16], mk_ref[:, :16]
    minus = jnp.full((count, 3), -1.0, bf16)
    pad_k = jnp.zeros((count, SPARE - 16 - 3), bf16)
    pad_v = jnp.zeros((count, SPARE - 3), bf16)
    key_grads, value_grads = [], []
    for h in range(heads):
        p = slice(h * HEAD_DIM, (h + 1) * HEAD_DIM)
        k, q, v, do = keys[:, p], queries[:, p], values[:, p], grads[:, p]
        inner = jnp.sum(do.astype(f32) * outs[:, p].astype(f32), axis=1, keepdims=True)
        ka = jnp.concatenate([k, mark_k, minus, pad_k], axis=1)
        qa = jnp.concatenate([q, mark_q] + split3(lse[:, h:h + 1] * (1.0 / SCALE)) + [pad_k], axis=1)
        va = jnp.concatenate([v, minus, pad_v], axis=1)
        da = jnp.concatenate([do] + split3(inner) + [pad_v], axis=1)
        kt = k.astype(f32).T.astype(bf16)
        total = jnp.zeros((HEAD_DIM, count), f32)
        kg, vg = [], []
        for b in range(count // block):
            r = slice(b * block, (b + 1) * block)
            probs = jnp.exp2(mm(ka[r], qa, NT) * factor)
            grad_scores = (probs * mm(va[r], da, NT)).astype(bf16)
            vg.append(mm(probs.astype(bf16), do))
            kg.append(mm(grad_scores, q))
            total = total + mm(kt[:, r], grad_scores)
        key_grads.append(jnp.concatenate(kg, axis=0) * SCALE)
        value_grads.append(jnp.concatenate(vg, axis=0))
        qt_ref[p, :] = total * SCALE
    query_grad = qt_ref[...].T.astype(bf16)
    value_grad = jnp.concatenate(value_grads, axis=1).astype(bf16)
    key_grad = jnp.concatenate(key_grads, axis=1).astype(bf16)
    full = jnp.concatenate([query_grad, key_grad, value_grad], axis=1)
    gn_ref[...] = full[:rows]
    gf_ref[...] = full[rows:]
    sum_ref[0:1, :] = jnp.sum(query_grad.astype(f32), axis=0, keepdims=True)
    sum_ref[1:2, :] = jnp.sum(value_grad.astype(f32), axis=0, keepdims=True)


def attend_back(order, pn, pf, grads, outs, ln, lf, mark_q, mark_k, **more):
    rows = pn.shape[0]
    cols = pn.shape[1] // 3
    count = 2 * rows
    return call(
        order, functools.partial(attend_back_kernel, block=rows),
        [shape((rows, 3 * cols), bf16)] * 2 + [Far(shape((2, cols), f32))],
        [Far(pn), Far(pf)] + list(grads) + [Far(x) for x in list(outs) + [ln, lf, mark_q, mark_k]], "attend_back",
        20 * count * count * cols, scratch=[pltpu.VMEM((cols, count), f32)], limit=14, **more)


def out_kernel(h, vec, a0, w0, a1, w1, a2, w2, a3, w3, res_ref, n_ref):
    total = h[...].astype(f32) + vec[OUT_BIAS:OUT_BIAS + 1, :]
    for a, w in ((a0, w0), (a1, w1), (a2, w2), (a3, w3)):
        total = total + mm(a[...], w[...])
    res_ref[...] = total
    leave(res_ref)
    unit, _ = unit_of(total)
    n_ref[...] = (unit * vec[GAIN2:GAIN2 + 1, :] + vec[SHIFT2:SHIFT2 + 1, :]).astype(bf16)


def out_project(order, h, vec, atts, ws, **more):
    rows, width = h.shape
    pairs = [Far(atts[0]), ws[0]]
    for a, w in zip(atts[1:], ws[1:]):
        pairs += [a, w]
    return call(
        order, out_kernel, [Far(shape((rows, width), f32)), shape((rows, width), bf16)],
        [Far(h), Far(vec)] + pairs, "out_project", 2 * rows * width * width, **more)


def gelu_both(pre):
    square = pre * pre
    tanh = jnp.tanh(GELU_A * pre * (1.0 + GELU_B * square))
    half = 0.5 * (1.0 + tanh)
    slope = half + 0.5 * pre * (1.0 - tanh * tanh) * (GELU_A * (1.0 + 3.0 * GELU_B * square))
    return pre * half, slope


def grad_act_kernel(ca, cb, w, out):
    rows = ca.shape[0]
    out[:rows] = mm(ca[...], w[...], NT)
    out[rows:] = mm(cb[...], w[...], NT)


def grad_act_of(order, ca, cb, w, **more):
    rows, width = ca.shape
    return call(order, grad_act_kernel, [shape((2 * rows, w.shape[0]), f32)], [ca, cb, w], "grad_act",
                4 * rows * width * w.shape[0], **more)[0]


def hidden_kernel(na, nb, ga, w, vec, act_ref, pre_ref, keep_ref, send_ref, sum_ref):
    rows = na.shape[0]
    sums = jnp.zeros(sum_ref.shape, f32)
    for i, n in enumerate((na, nb)):
        r = slice(i * rows, (i + 1) * rows)
        pre = mm(n[...], w[...], NT) + vec[UP_BIAS:UP_BIAS + 1, :w.shape[0]]
        act, slope = gelu_both(pre)
        act_ref[r] = act.astype(bf16)
        grad = (ga[r] * slope).astype(bf16)
        pre_ref[r] = grad
        sums = sums + jnp.sum(grad.astype(f32), axis=0, keepdims=True)
    sum_ref[...] = sums
    keep_ref[...] = mm(pre_ref[:rows], w[...])
    leave(keep_ref)
    send_ref[...] = mm(pre_ref[rows:], w[...]).astype(bf16)


def hidden(order, na, nb, ga, w, vec, far_keep, **more):
    rows, width = na.shape
    units = w.shape[0]
    keep = shape((rows, width), f32)
    return call(
        order, hidden_kernel,
        [shape((2 * rows, units), bf16)] * 2
        + [Far(keep) if far_keep else keep, shape((rows, width), bf16), Far(shape((1, units), f32))],
        [na, nb, ga, w, Far(vec)], "hidden", 8 * rows * width * units, **more)


def down_kernel(act, w, keep_ref, send_ref):
    rows = keep_ref.shape[0]
    keep_ref[...] = mm(act[:rows], w[...])
    leave(keep_ref)
    send_ref[...] = mm(act[rows:], w[...]).astype(bf16)


def down(order, act, w, far_keep, **more):
    rows, units = act.shape
    width = w.shape[1]
    keep = shape((rows // 2, width), f32)
    return call(order, down_kernel, [Far(keep) if far_keep else keep, shape((rows // 2, width), bf16)], [act, w],
                "down", 2 * rows * width * units, **more)


def insert_bit(j, bit, value):
    low = bit - 1
    return (j // bit) * (2 * bit) + value * bit + (j & low)


SMALL = 16
TOP_ROW = 9
CHUNK = 384


def put_small(ref, base, small):
    for c in range(small.shape[1] // CHUNK):
        part = small[:, c * CHUNK:(c + 1) * CHUNK]
        high = part.astype(bf16)
        at = base + 2 * SMALL * c
        ref[at:at + SMALL, :CHUNK] = high
        ref[at + SMALL:at + 2 * SMALL, :CHUNK] = (part - high.astype(f32)).astype(bf16)


def add_small(small, ref, base):
    parts = []
    for c in range(small.shape[1] // CHUNK):
        at = base + 2 * SMALL * c
        parts.append(ref[at:at + SMALL, :CHUNK].astype(f32) + ref[at + SMALL:at + 2 * SMALL, :CHUNK].astype(f32))
    other = jnp.concatenate(parts, axis=1)
    is_top = lax.broadcasted_iota(jnp.int32, small.shape, 0) == TOP_ROW
    return jnp.where(is_top, jnp.maximum(small, other), small + other)


def weight_small_kernel(mine_ref, xn, xf, gn, gf, sn, sf, sb, un, uf, qv, tn, tf,
                        keep_ref, send_ref, small_ref, lt_ref, acc_ref, *, first, stop, bit):
    kept, block, cols = keep_ref.shape
    rows = xn.shape[0]
    lt_ref[:, :rows] = xn[...].T
    lt_ref[:, rows:] = xf[...].T
    acc_ref[...] = mm(lt_ref[...], jnp.concatenate([gn[:, first:stop], gf[:, first:stop]], axis=0))
    mine = mine_ref[0]
    for j in range(kept):
        at = pl.multiple_of(insert_bit(j, bit, mine) * block, block)
        keep_ref[j] = acc_ref[pl.ds(at, block), :].astype(bf16)
        at = pl.multiple_of(insert_bit(j, bit, 1 - mine) * block, block)
        send_ref[j * block:(j + 1) * block, :] = acc_ref[pl.ds(at, block), :].astype(bf16)
    small_ref[...] = jnp.zeros(small_ref.shape, f32)
    small_ref[0:2, :] = sn[...] + sf[...]
    small_ref[2:6, :] = sb[...]
    small_ref[6:7, :un.shape[1]] = un[...] + uf[...]
    small_ref[7:9, :qv.shape[1]] = qv[...]
    small_ref[TOP_ROW:TOP_ROW + 1, :tn.shape[1]] = jnp.maximum(tn[...], tf[...])
    put_small(send_ref, kept * block, small_ref[...])


def weight_small(order, lefts, rights, smalls, first, stop, mine, bit, parts, name, **more):
    rows, width = lefts[0].shape
    block, cols = width // parts, stop - first
    extra = width // CHUNK * 2 * SMALL
    return call(
        order, functools.partial(weight_small_kernel, first=first, stop=stop, bit=bit),
        [shape((parts // 2, block, cols), bf16), shape((parts // 2 * block + extra, cols), bf16),
         shape((SMALL, width), f32)],
        [mine] + list(lefts) + list(rights) + [Far(x) for x in smalls], name, 4 * width * rows * cols,
        scratch=[pltpu.VMEM((width, 2 * rows), bf16), pltpu.VMEM((width, cols), f32)], smem=1, **more)


def fold_small_kernel(mine_ref, keep_ref, got_ref, small_ref, nk_ref, ns_ref, new_ref, *, bit):
    mine = mine_ref[0]
    parts, block, cols = keep_ref.shape
    kept = nk_ref.shape[0]
    for j in range(kept):
        for side in (0, 1):
            at = insert_bit(j, bit, mine if side == 0 else 1 - mine)
            start = pl.multiple_of(at * block, block)
            total = (keep_ref[at].astype(f32) + got_ref[pl.ds(start, block), :].astype(f32)).astype(bf16)
            if side == 0:
                nk_ref[j] = total
            else:
                ns_ref[j * block:(j + 1) * block, :] = total
    new_ref[...] = add_small(small_ref[...], got_ref, parts * block)
    put_small(ns_ref, kept * block, new_ref[...])


def fold_small(order, keep, got, small, mine, bit, **more):
    parts, block, cols = keep.shape
    extra = got.shape[0] - parts * block
    return call(
        order, functools.partial(fold_small_kernel, bit=bit),
        [shape((parts // 2, block, cols), bf16), shape((parts // 2 * block + extra, cols), bf16),
         shape(small.shape, f32)], [mine, keep, got, small], "fold_small", 2 * keep.size, smem=1, **more)


def weight_kernel(mine_ref, *refs, groups, bit, tile):
    keep_ref, send_ref, lt_ref, acc_ref = refs[-4:]
    kept, block, cols = keep_ref.shape
    products = []
    at = 0
    for lefts, rights, first, stop in groups:
        start = 0
        for x in refs[at:at + lefts]:
            n = x.shape[0]
            lt_ref[:, start:start + n] = x[...].T
            start += n
        at += lefts
        right = [x[:, first:stop] for x in refs[at:at + rights]]
        at += rights
        right = jnp.concatenate(right, axis=0) if rights > 1 else right[0]
        if len(groups) > 1:
            products.append(mm(lt_ref[...], right))
    mine = mine_ref[0]
    for c0 in range(0, cols, tile):
        c1 = min(cols, c0 + tile)
        if products:
            acc_ref[:, :c1 - c0] = jnp.concatenate(products, axis=1)
        else:
            acc_ref[:, :c1 - c0] = mm(lt_ref[...], right[:, c0:c1])
        for j in range(kept):
            for ref, side in ((keep_ref, mine), (send_ref, 1 - mine)):
                row_at = pl.multiple_of(insert_bit(j, bit, side) * block, block)
                ref[j, :, c0:c1] = acc_ref[pl.ds(row_at, block), :c1 - c0].astype(bf16)


def weight_grad(order, groups, mine, bit, parts, name, tile=384, **more):
    width = groups[0][0][0].shape[1]
    count = sum(x.shape[0] for x in groups[0][0])
    cols = sum(stop - first for _, _, first, stop in groups)
    block = width // parts
    if len(groups) > 1:
        tile = cols
    ins = [mine]
    for lefts, rights, _, _ in groups:
        ins += list(lefts) + list(rights)
    sizes = tuple((len(lefts), len(rights), first, stop) for lefts, rights, first, stop in groups)
    return call(
        order, functools.partial(weight_kernel, groups=sizes, bit=bit, tile=tile),
        [shape((parts // 2, block, cols), bf16)] * 2, ins, name, 2 * width * count * cols,
        scratch=[pltpu.VMEM((width, count), bf16), pltpu.VMEM((width, min(tile, cols)), f32)], smem=1, **more)


def fold_kernel(mine_ref, keep_ref, got_ref, nk_ref, ns_ref, *, bit):
    mine = mine_ref[0]
    for j in range(nk_ref.shape[0]):
        for ref, side in ((nk_ref, mine), (ns_ref, 1 - mine)):
            at = insert_bit(j, bit, side)
            ref[j] = (keep_ref[at].astype(f32) + got_ref[at].astype(f32)).astype(bf16)


def fold(order, keep, got, mine, bit, **more):
    parts, block, cols = keep.shape
    return call(order, functools.partial(fold_kernel, bit=bit), [shape((parts // 2, block, cols), bf16)] * 2,
                [mine, keep, got], "fold", 2 * keep.size, smem=1, **more)


def join_kernel(a, b, out):
    out[...] = (a[...] + b[...].astype(f32)).astype(bf16)


def join(order, a, b, **more):
    return call(order, join_kernel, [shape(a.shape, bf16)], [a, b], "join", a.size, **more)[0]


def finish_kernel(keep_ref, got_ref, out_ref):
    out_ref[...] = keep_ref[0].astype(f32) + got_ref[0].astype(f32)


def finish(order, keep, got, **more):
    return call(order, finish_kernel, [shape(keep.shape[1:], f32)], [keep, got], "finish", keep.size, **more)[0]


def split_kernel(ka, ga, small, kb, gb, qkv_ref, out_ref, new_ref):
    block = ka.shape[1]
    new_ref[...] = add_small(small[...], ga, block)
    whole = jnp.concatenate(
        [ka[0].astype(f32) + ga[:block, :].astype(f32), kb[0].astype(f32) + gb[0].astype(f32)], axis=1)
    cols = out_ref.shape[1]
    for i in range(3):
        qkv_ref[i] = whole[:, i * cols:(i + 1) * cols]
    out_ref[...] = whole[:, 3 * cols:]


def finish_split(order, ka, ga, small, kb, gb, cols, **more):
    rows = ka.shape[1]
    return call(
        order, split_kernel,
        [shape((3, rows, cols), f32), shape((rows, cols), f32), shape(small.shape, f32)],
        [ka, ga, small, kb, gb], "finish_split", ka.size, **more)


def mid_kernel(res, cot, vec, g0, r1, ry, w0, w1, w2, w3, gr_ref, gb_ref, a0, a1, a2, a3, sum_ref):
    unit, inverse = unit_of(res[...])
    top = cot[...].astype(f32)
    grad = g0[...] + r1[...].astype(f32) + ry[...].astype(f32)
    resid = top + norm_back(grad, unit, inverse, vec[GAIN2:GAIN2 + 1, :])
    gr_ref[...] = resid
    leave(gr_ref)
    branch = resid.astype(bf16)
    gb_ref[...] = branch
    for a, w in ((a2, w2), (a3, w3), (a1, w1), (a0, w0)):
        a[...] = mm(branch, w[...], NT).astype(bf16)
    for i, x in enumerate((resid, grad * unit, grad, top)):
        sum_ref[i:i + 1, :] = jnp.sum(x, axis=0, keepdims=True)


def mid(order, res, cot, vec, g0, r1, ry, ws, **more):
    rows, width = g0.shape
    cols = ws[0].shape[0]
    return call(
        order, mid_kernel,
        [Far(shape((rows, width), f32)), shape((rows, width), bf16)] + [shape((rows, cols), bf16)] * 4
        + [Far(shape((4, width), f32))],
        [Far(res), Far(cot), Far(vec), Far(g0), r1, ry] + list(ws), "mid", 2 * rows * width * width, **more)


def grad_norm_kernel(g, w, xa, xb, keep_ref, send_ref, sum_ref):
    rows = xa.shape[0]
    sums = [0.0, 0.0]
    for i, (x, ref) in enumerate(((xa, keep_ref), (xb, send_ref))):
        r = slice(i * rows, (i + 1) * rows)
        grad = mm(g[r], w[...])
        ref[...] = grad.astype(ref.dtype)
        leave(ref)
        unit, _ = unit_of(x[...].astype(f32))
        sums[0] = sums[0] + jnp.sum(grad * unit, axis=0, keepdims=True)
        sums[1] = sums[1] + jnp.sum(grad, axis=0, keepdims=True)
    sum_ref[0:1, :] = sums[0]
    sum_ref[1:2, :] = sums[1]


def grad_norm(order, g, w, xa, xb, far_keep, **more):
    rows, width = xa.shape
    keep = shape((rows, width), f32)
    return call(
        order, grad_norm_kernel,
        [Far(keep) if far_keep else keep, shape((rows, width), bf16), Far(shape((2, width), f32))],
        [g, w, Far(xa), Far(xb)], "grad_norm", 4 * rows * width * g.shape[1], **more)


def last_kernel(x, gr, vec, g0, r1, ry, out):
    unit, inverse = unit_of(x[...].astype(f32))
    grad = g0[...] + r1[...].astype(f32) + ry[...].astype(f32)
    out[...] = (gr[...] + norm_back(grad, unit, inverse, vec[GAIN1:GAIN1 + 1, :])).astype(bf16)


def last(order, x, gr, vec, g0, r1, ry, **more):
    return call(order, last_kernel, [Far(shape(x.shape, bf16))], [Far(x), Far(gr), Far(vec), Far(g0), r1, ry], "last",
                20 * x.size, **more)[0]


def make_local(dp_size, tensor_size):
    def scatter_plain(groups):
        index = lax.axis_index("dp")
        value = jnp.concatenate(
            [mm(jnp.concatenate(lefts), jnp.concatenate([x[:, first:stop] for x in rights]), TN)
             for lefts, rights, first, stop in groups], axis=1).astype(bf16)
        width, cols = value.shape
        block = width // dp_size
        bit = 1
        while bit < dp_size:
            count = value.shape[0] // block // 2
            pairs = value.reshape(count, 2, block, cols)
            mine = (index // bit) % 2
            keep = lax.dynamic_index_in_dim(pairs, mine, 1, keepdims=False)
            send = lax.dynamic_index_in_dim(pairs, 1 - mine, 1, keepdims=False)
            value = keep.astype(f32) + swap(send, "dp", dp_size, bit).astype(f32)
            bit *= 2
            if bit < dp_size:
                value = value.astype(bf16)
            value = value.reshape(count * block, cols)
        return value

    class Spread:
        def __init__(self, order, groups, bits, name, **more):
            width = groups[0][0][0].shape[1]
            self.order, self.bits, self.index = order, bits, lax.axis_index("dp")
            self.paired = dp_size == 8 and (width // dp_size) % 16 == 0
            if self.paired:
                self.step = 0
                self.keep, send = weight_grad(order, groups, self.mine(bits[0]), bits[0], dp_size, name, **more)
                self.got = swap(after(send, order.last), "dp", dp_size, bits[0])
            else:
                self.value = scatter_plain(groups)

        def mine(self, bit):
            return ((self.index // bit) % 2).astype(jnp.int32).reshape(1)

        def local_bit(self):
            bit = local = self.bits[self.step]
            for used in self.bits[:self.step]:
                if used < bit:
                    local //= 2
            return bit, local

        def fold(self, **more):
            if self.paired:
                self.step += 1
                bit, local_bit = self.local_bit()
                self.keep, send = fold(self.order, self.keep, self.got, self.mine(bit), local_bit, **more)
                self.got = swap(after(send, self.order.last), "dp", dp_size, bit)

        def result(self, **more):
            if self.paired:
                return finish(self.order, self.keep, self.got, **more)
            return self.value

    class SpreadSmall(Spread):
        def __init__(self, order, lefts, rights, smalls, first, stop, bits, name, **more):
            width = lefts[0].shape[1]
            self.order, self.bits, self.index, self.step = order, bits, lax.axis_index("dp"), 0
            self.keep, send, self.small = weight_small(
                order, lefts, rights, smalls, first, stop, self.mine(bits[0]), bits[0], dp_size, name, **more)
            self.got = swap(after(send, order.last), "dp", dp_size, bits[0])

        def fold(self, **more):
            self.step += 1
            bit, local_bit = self.local_bit()
            self.keep, send, self.small = fold_small(
                self.order, self.keep, self.got, self.small, self.mine(bit), local_bit, **more)
            self.got = swap(after(send, self.order.last), "dp", dp_size, bit)

    def local(hidden_in, picture_ids, norm1_gain, norm1_bias, w_qkv, qv_bias, w_out, out_bias,
              norm2_gain, norm2_bias, w_up, up_bias, w_down, down_bias, cotangent):
        rows, width = hidden_in.shape
        head_width = w_qkv.shape[2]
        place = lax.axis_index("tensor")
        order = Order()
        units = w_up.shape[1]
        wt_qkv = w_qkv.transpose(0, 2, 1).reshape(3 * head_width, width)
        wt_up = w_up.T
        bias_qkv = jnp.concatenate([qv_bias[0], jnp.zeros_like(qv_bias[0]), qv_bias[1]])
        vec = jnp.stack([jnp.pad(x, (0, width - x.shape[0])) for x in (
            norm1_gain, norm1_bias, norm2_gain, norm2_bias, out_bias, up_bias, bias_qkv, down_bias)])
        index = lax.axis_index("dp")

        def pin(value):
            return value if order.last is None else after(value, order.last)

        def core(value):
            return swap(pin(value), "tensor", tensor_size, 1)

        def across(value):
            return swap(pin(value), "tensor", tensor_size, 2)

        def diagonal(value):
            return swap(pin(value), "tensor", tensor_size, 3)

        def double(value, bit):
            other = swap(pin(value), "dp", dp_size, bit)
            low = (index // bit) % 2 == 0
            return jnp.concatenate([jnp.where(low, value, other), jnp.where(low, other, value)])

        quarters = dp_size % 4 == 0 and head_width % 32 == 0
        quarter = head_width // 4 if quarters else head_width
        paired = dp_size == 8 and (width // dp_size) % 16 == 0
        h2 = across(hidden_in)
        h1, c1 = core(hidden_in), core(cotangent)
        w2 = across(lax.dynamic_slice_in_dim(w_out, (index % 4) * quarter, quarter) if quarters else w_out)
        w1 = core(w_out)
        if quarters:
            w2 = double(w2, 1)
            w2 = double(w2, 2)
        w3 = core(w2)
        ws = [w_out, w1, w2, w3]
        mark_q, mark_k = marks(order, place.astype(jnp.int32).reshape(1), picture_ids.reshape(tensor_size, rows))
        nn, pn, pn_far = qkv(order, hidden_in, h1, vec, wt_qkv)
        h3 = core(h2)
        c2 = across(after(cotangent, h2))
        nf, pf, pf_far = qkv(order, h2, h3, vec, wt_qkv)
        a2, a3, lse_f, top_f = attend(order, pf, pn, pf, mark_q, mark_k, 2 * rows, waits=[w1, c1])
        got2, got3 = across(a2), diagonal(a3)
        a0, a1, lse_n, top_n = attend(order, pn, pn, pf, mark_q, mark_k, 0, waits=[w3])
        got1, c3 = core(a1), core(c2)
        ga_n = grad_act_of(order, cotangent, c1, w_down, waits=[c2, got2, got3])
        residual, normed_b = out_project(order, hidden_in, vec, [a0, got1, got2, got3], ws)
        b2, b1 = across(normed_b), core(normed_b)
        ga_f = grad_act_of(order, c2, c3, w_down)
        act_n, pre_n, g0, g1, up_n = hidden(order, normed_b, b1, ga_n, wt_up, vec, True)
        b3, r1 = core(b2), core(g1)
        act_f, pre_f, g2, g3, up_f = hidden(order, b2, b3, ga_f, wt_up, vec, False)
        r3 = core(g3)
        m0, m1 = down(order, act_n, w_down, True, waits=[r1])
        n1 = core(m1)
        ry = across(join(order, g2, r3))
        s_up = Spread(order, [([normed_b, b1, b2, b3], [pre_n, pre_f], 0, units)], (1, 2, 4), "weight_up")
        s_down = Spread(order, [([cotangent, c1, c2, c3], [act_n, act_f], 0, units)], (2, 1, 4), "weight_down",
                        waits=[n1])
        grad_resid, branch, p0, p1, p2, p3, sums_b = mid(order, residual, cotangent, vec, g0, r1, ry, ws)
        d = [p0, core(p1), across(p2), diagonal(p3)]
        m2, m3 = down(order, act_f, w_down, False)
        n3 = core(m3)
        s_up.fold()
        s_down.fold()
        n2 = join(order, m2, n3)
        gb2 = across(after(branch, d[2], d[3]))
        gq_n, gq_f, sums_qv = attend_back(
            order, pn_far, pf_far, d, [a0, a1, a2, a3], lse_n, lse_f, mark_q, mark_k)
        gb3, gb1 = core(gb2), core(branch)
        s_up.fold()
        s_down.fold()
        e2, e3, sums_f = grad_norm(order, gq_f, wt_qkv, h2, h3, False)
        f3 = core(e3)
        cut = 512 if paired else head_width
        s_vo = Spread(order, [([nn, nf], [gq_n, gq_f], cut, 3 * head_width),
                              ([branch, gb1, gb2, gb3], [a0, a1, a2, a3], 0, head_width)], (1, 2, 4), "weight_vo")
        fy = across(join(order, e2, f3))
        e0, e1, sums_n = grad_norm(order, gq_n, wt_qkv, hidden_in, h1, True)
        f1 = core(e1)
        smalls = [sums_n, sums_f, sums_b, up_n, up_f, sums_qv, top_n, top_f]
        if paired:
            s_qk = SpreadSmall(order, [nn, nf], [gq_n, gq_f], smalls, 0, cut, (2, 1, 4), "weight_qk")
        else:
            s_qk = Spread(order, [([nn, nf], [gq_n, gq_f], 0, cut)], (2, 1, 4), "weight_qk")
        g_up = s_up.result()
        g_down = s_down.result(waits=[f1])
        ny = across(after(n2, fy))
        s_vo.fold()
        grad_in = last(order, hidden_in, grad_resid, vec, e0, f1, fy)
        s_qk.fold()
        s_vo.fold()
        s_qk.fold()
        hidden_out = (residual + m0 + n1.astype(f32) + ny.astype(f32) + down_bias).astype(bf16)
        if paired:
            g_qkv, g_out, small = finish_split(order, s_qk.keep, s_qk.got, s_qk.small, s_vo.keep, s_vo.got, head_width,
                                               waits=[hidden_out])
        else:
            last_w = jnp.concatenate([s_qk.result(), s_vo.result()], axis=1)
            g_qkv = jnp.stack([last_w[:, i * head_width:(i + 1) * head_width] for i in range(3)])
            g_out = last_w[:, 3 * head_width:]
            wide = lambda x: jnp.pad(x, ((0, 0), (0, width - x.shape[1])))
            small = jnp.concatenate([sums_n + sums_f, sums_b, wide(up_n + up_f), wide(sums_qv),
                                     wide(jnp.maximum(top_n, top_f))])
            bit = 1
            while bit < dp_size:
                other = swap(small, "dp", dp_size, bit)
                small = jnp.concatenate([small[:TOP_ROW] + other[:TOP_ROW], jnp.maximum(small[TOP_ROW:], other[TOP_ROW:])])
                bit *= 2
        shared = small[:8]
        shared = shared + swap(shared, "tensor", tensor_size, 1)
        shared = shared + swap(shared, "tensor", tensor_size, 2)
        top = small[TOP_ROW, :head_width // HEAD_DIM]
        limit = jnp.float32(CLIP_LIMIT)
        factor = jnp.sqrt(limit / jnp.maximum(top, limit))
        column = jnp.repeat(factor, HEAD_DIM)
        scaled_qk = (w_qkv[:2].astype(f32) * column).astype(bf16)
        scaled_query_bias = qv_bias[0] * column
        return (hidden_out, grad_in, g_qkv, g_out.T, g_up, g_down.T, small[7:9, :head_width], small[6, :units],
                shared[:6], top, scaled_qk, scaled_query_bias)

    return local


def solution(mesh):
    return jax.shard_map(
        make_local(mesh.shape["dp"], mesh.shape["tensor"]),
        mesh=mesh,
        in_specs=(
            P(("dp", "tensor"), None), P("dp"), P(), P(), P(None, None, "tensor"), P(None, "tensor"),
            P("tensor", None), P(), P(), P(), P(None, "tensor"), P("tensor"), P("tensor", None), P(),
            P(("dp", "tensor"), None),
        ),
        out_specs=(
            P(("dp", "tensor"), None), P(("dp", "tensor"), None), P(None, "dp", "tensor"), P("tensor", "dp"),
            P("dp", "tensor"), P("tensor", "dp"), P(None, "tensor"), P("tensor"), P(), P("tensor"),
            P(None, None, "tensor"), P("tensor"),
        ),
        check_vma=False,
    )
```

```python
import functools
import math

import jax
import jax.numpy as jnp
from jax import lax
from jax.experimental import pallas as pl
from jax.experimental.pallas import tpu as pltpu
from jax.sharding import PartitionSpec as P

HEAD_DIM = 72
PACK = 1024
CLIP_LIMIT = 9
LANES = 128
SPARE = LANES - HEAD_DIM
SCALE = HEAD_DIM ** (-0.5)
LOG2E = 1.4426950408889634
GELU_A = 0.7978845608028654
GELU_B = 0.044715

eps_norm = 1e-06
neg_fill = -1e30
f32 = jnp.float32
bf16 = jnp.bfloat16
NN = (((1,), (0,)), ((), ()))
NT = (((1,), (1,)), ((), ()))
TN = (((0,), (0,)), ((), ()))


def mm(left, right, dims=NN):
    return lax.dot_general(left, right, dims, preferred_element_type=f32)


def swap(value, axis, size, bit):
    return lax.ppermute(value, axis, [(i, i ^ bit) for i in range(size)])


def after(value, *others):
    return lax.optimization_barrier((value,) + others)[0]


class Far:
    def __init__(self, value):
        self.value = value


class Lazy:
    def __init__(self, ref, copy):
        self.ref, self.copy, self.shape, self.dtype = ref, copy, ref.shape, ref.dtype

    def __getitem__(self, index):
        if self.copy is not None:
            self.copy.wait()
            self.copy = None
        return self.ref[index]


class Out:
    def __init__(self, ref, copy):
        self.ref, self.copy, self.shape, self.dtype, self.left = ref, copy, ref.shape, ref.dtype, False

    def __getitem__(self, index):
        return self.ref[index]

    def __setitem__(self, index, value):
        self.ref[index] = value

    def leave(self):
        if not self.left:
            self.copy.start()
            self.left = True


def leave(ref):
    if isinstance(ref, Out):
        ref.leave()


class Order:
    def __init__(self):
        self.last = None


def call(order, kernel, outs, ins, name, flops, scratch=(), limit=9, smem=0, waits=()):
    near = pl.BlockSpec(memory_space=pltpu.VMEM)
    far = pl.BlockSpec(memory_space=pltpu.HBM)
    scalar = pl.BlockSpec(memory_space=pltpu.SMEM)
    in_far = [isinstance(x, Far) for x in ins]
    out_far = [isinstance(x, Far) for x in outs]
    ins = [x.value if isinstance(x, Far) else x for x in ins]
    outs = [x.value if isinstance(x, Far) else x for x in outs]
    moved = sum(x.size * x.dtype.itemsize for x in outs + ins)
    unread = ([] if order.last is None else [order.last]) + list(waits)
    count, extra = len(ins), len(scratch)
    buffers = [pltpu.VMEM(x.shape, x.dtype) for x, f in zip(ins + outs, in_far + out_far) if f]

    def body(*refs):
        in_refs, refs = refs[:count], refs[count + len(unread):]
        out_refs, refs = refs[:len(outs)], refs[len(outs) + 1:]
        own, refs = refs[:extra], refs[extra:]
        buffer_refs, sems = list(refs[:len(buffers)]), refs[len(buffers):]
        slot = 0
        given, leaving = [], []
        for ref, f in zip(in_refs, in_far):
            if f:
                copy = pltpu.make_async_copy(ref, buffer_refs[slot], sems[0].at[slot])
                copy.start()
                ref = Lazy(buffer_refs[slot], copy)
                slot += 1
            given.append(ref)
        for ref, f in zip(out_refs, out_far):
            if f:
                ref = Out(buffer_refs[slot], pltpu.make_async_copy(buffer_refs[slot], ref, sems[0].at[slot]))
                leaving.append(ref)
                slot += 1
            given.append(ref)
        kernel(*given, *own)
        for ref in given:
            if isinstance(ref, Lazy) and ref.copy is not None:
                ref.copy.wait()
        for ref in leaving:
            ref.leave()
        for ref in leaving:
            ref.copy.wait()

    size = sum(math.prod(x.shape) * x.dtype.itemsize for x, f in zip(ins + outs, in_far + out_far) if f)
    results = pl.pallas_call(
        body,
        out_shape=tuple(pltpu.HBM(x.shape, x.dtype) if f else x for x, f in zip(outs, out_far))
        + (pltpu.HBM((8, LANES), f32),),
        in_specs=[scalar] * smem + [far if f else near for f in in_far[smem:]] + [pl.BlockSpec(memory_space=pl.ANY)] * len(unread),
        out_specs=tuple(far if f else near for f in out_far) + (far,),
        scratch_shapes=list(scratch) + buffers + ([pltpu.SemaphoreType.DMA((len(buffers),))] if buffers else []),
        compiler_params=pltpu.CompilerParams(vmem_limit_bytes=limit * 2**20 + size + size // 4),
        cost_estimate=pl.CostEstimate(flops=int(flops), bytes_accessed=int(moved), transcendentals=0),
        name=name,
    )(*(pltpu.with_memory_space_constraint(x, pltpu.HBM) if f else x for x, f in zip(ins, in_far)), *(pltpu.with_memory_space_constraint(x, pltpu.HBM) if i == 0 and order.last is not None else x
                                                                              for i, x in enumerate(unread)))
    order.last = results[-1]
    return results[:-1]


def shape(dims, dtype):
    return jax.ShapeDtypeStruct(tuple(dims), dtype)


def row(vector):
    return vector.reshape(1, -1)


def unit_of(values_in):
    row_mean = jnp.mean(values_in, axis=-1, keepdims=True)
    centred = values_in - row_mean
    variance = jnp.mean(centred * centred, axis=-1, keepdims=True)
    inverse = lax.rsqrt(variance + eps_norm)
    return centred * inverse, inverse


def norm_back(grad_rows, unit_rows, inverse, gain):
    scaled = grad_rows * gain
    return inverse * (
        scaled
        - jnp.mean(scaled, axis=-1, keepdims=True)
        - unit_rows * jnp.mean(scaled * unit_rows, axis=-1, keepdims=True)
    )


GAIN1, SHIFT1, GAIN2, SHIFT2, OUT_BIAS, UP_BIAS, QKV_BIAS, DOWN_BIAS = range(8)


def qkv_kernel(vec, xa, xb, w, n_ref, p_ref, copy_ref):
    rows = xa.shape[0]
    cols = w.shape[0]
    for i, x in enumerate((xa, xb)):
        unit, _ = unit_of(x[...].astype(f32))
        n_ref[i * rows:(i + 1) * rows, :] = (
            unit * vec[GAIN1:GAIN1 + 1, :] + vec[SHIFT1:SHIFT1 + 1, :]).astype(bf16)
    leave(n_ref)
    p_ref[...] = (mm(n_ref[...], w[...], NT) + vec[QKV_BIAS:QKV_BIAS + 1, :cols]).astype(bf16)
    copy_ref[...] = p_ref[...]


def qkv(order, xa, xb, vec, w, **more):
    rows, width = xa.shape
    cols = w.shape[0]
    return call(
        order, qkv_kernel,
        [Far(shape((2 * rows, width), bf16)), shape((2 * rows, cols), bf16), Far(shape((2 * rows, cols), bf16))],
        [Far(vec), xa, xb, w], "qkv", 4 * rows * width * cols, **more)


def marks_kernel(place_ref, ids_ref, g1, s1, g2, s2, ob, ub, qv, db, q_ref, k_ref, vec_ref):
    rows = ids_ref.shape[1]
    lane = lax.broadcasted_iota(jnp.int32, (LANES, rows), 0)
    for slot in range(ids_ref.shape[0]):
        ids = ids_ref[pl.ds(place_ref[0] ^ slot, 1), :]
        same = jnp.where((ids + 1) == lane, 1.0, 0.0).T[:, :SPARE]
        r = slice(slot * rows, (slot + 1) * rows)
        q_ref[r, :] = same.astype(bf16)
        k_ref[r, :] = jnp.where(same > 0.5, 0.0, neg_fill).astype(bf16)
    for i, x in ((GAIN1, g1), (SHIFT1, s1), (GAIN2, g2), (SHIFT2, s2), (OUT_BIAS, ob), (UP_BIAS, ub), (DOWN_BIAS, db)):
        vec_ref[i:i + 1, :x.shape[0]] = x[...].reshape(1, x.shape[0])
    cols = qv.shape[1]
    biases = jnp.concatenate([qv[0:1, :], jnp.zeros((1, cols), f32), qv[1:2, :]], axis=1)
    vec_ref[QKV_BIAS:QKV_BIAS + 1, :3 * cols] = biases


def marks(order, place, ids, vectors):
    width = vectors[0].shape[0]
    return call(order, marks_kernel,
                [Far(x) for x in [shape((ids.size, SPARE), bf16)] * 2 + [shape((8, width), f32)]],
                [place, ids] + [Far(x) for x in vectors], "marks", ids.size, smem=1)


def attend_kernel(p_ref, kn, kf, mark_q, mark_k, oa_ref, ob_ref, lse_ref, top_ref, *, block, first):
    rows = p_ref.shape[0]
    cols = oa_ref.shape[1]
    heads = cols // HEAD_DIM
    factor = SCALE * LOG2E
    keys = jnp.concatenate([kn[:, cols:], kf[:, cols:]], axis=0)
    marked = mark_k[...]
    ones = jnp.where(lax.broadcasted_iota(jnp.int32, marked.shape, 1) == 0, 1.0, 0.0).astype(bf16)
    parts = [slice(h * HEAD_DIM, (h + 1) * HEAD_DIM) for h in range(heads)]
    ka = [jnp.concatenate([keys[:, p], marked], axis=1) for p in parts]
    va = [jnp.concatenate([keys[:, cols + p.start:cols + p.stop], ones], axis=1) for p in parts]
    qa = [jnp.concatenate([p_ref[:, p], mark_q[first:first + rows, :]], axis=1) for p in parts]
    blocks = rows // block
    steps = [(h, b) for h in range(heads) for b in range(blocks)]

    def score(i):
        h, b = steps[i]
        return mm(qa[h][b * block:(b + 1) * block], ka[h], NT)

    outs, lses, tops = {}, {}, {}
    ahead = score(0)
    for i, (h, b) in enumerate(steps):
        scores = ahead
        if i + 1 < len(steps):
            ahead = score(i + 1)
        top = jnp.max(scores, axis=1, keepdims=True)
        probs = jnp.exp2(scores * factor - top * factor).astype(bf16)
        out = mm(probs, va[h])
        total = out[:, HEAD_DIM:HEAD_DIM + 1]
        outs[h, b] = out[:, :HEAD_DIM] * (1.0 / total)
        lses[h, b] = top * SCALE + jnp.log(total)
        tops.setdefault(h, []).append(jnp.max(top, axis=0, keepdims=True))
    flat = [jnp.concatenate([outs[h, b] for h in range(heads)], axis=1).astype(bf16) for b in range(blocks)]
    half = blocks // 2
    oa_ref[...] = jnp.concatenate(flat[:half], axis=0)
    ob_ref[...] = jnp.concatenate(flat[half:], axis=0)
    for b in range(blocks):
        lse_ref[b * block:(b + 1) * block, :] = jnp.concatenate([lses[h, b] for h in range(heads)], axis=1)
    top_ref[...] = jnp.concatenate([functools.reduce(jnp.maximum, tops[h]) * SCALE for h in range(heads)], axis=1)


def attend(order, p, pn, pf, mark_q, mark_k, first, **more):
    rows = p.shape[0]
    cols = p.shape[1] // 3
    count = mark_k.shape[0]
    heads = cols // HEAD_DIM
    return call(
        order, functools.partial(attend_kernel, block=rows // 2, first=first),
        [Far(x) for x in [shape((rows // 2, cols), bf16)] * 2 + [shape((rows, heads), f32), shape((1, heads), f32)]],
        [p, pn, pf, Far(mark_q), Far(mark_k)], "attend", 8 * rows * count * cols, **more)


def split3(value):
    high = value.astype(bf16)
    rest = value - high.astype(f32)
    middle = rest.astype(bf16)
    return [high, middle, (rest - middle.astype(f32)).astype(bf16)]


def attend_back_kernel(*refs, block):
    (pn, pf, d0, d1, d2, d3, a0, a1, a2, a3, ln, lf, mq_ref, mk_ref,
     gn_ref, gf_ref, sum_ref, qt_ref) = refs
    rows = pn.shape[0]
    cols = d0.shape[1]
    count = 2 * rows
    heads = cols // HEAD_DIM
    factor = SCALE * LOG2E
    cat = lambda *xs: jnp.concatenate([x[...] for x in xs], axis=0)
    whole = cat(pn, pf)
    queries, keys, values = whole[:, :cols], whole[:, cols:2 * cols], whole[:, 2 * cols:]
    grads, outs, lse = cat(d0, d1, d2, d3), cat(a0, a1, a2, a3), cat(ln, lf)
    mark_q, mark_k = mq_ref[:, :16], mk_ref[:, :16]
    minus = jnp.full((count, 3), -1.0, bf16)
    pad_k = jnp.zeros((count, SPARE - 16 - 3), bf16)
    pad_v = jnp.zeros((count, SPARE - 3), bf16)
    key_grads, value_grads = [], []
    for h in range(heads):
        p = slice(h * HEAD_DIM, (h + 1) * HEAD_DIM)
        k, q, v, do = keys[:, p], queries[:, p], values[:, p], grads[:, p]
        inner = jnp.sum(do.astype(f32) * outs[:, p].astype(f32), axis=1, keepdims=True)
        ka = jnp.concatenate([k, mark_k, minus, pad_k], axis=1)
        qa = jnp.concatenate([q, mark_q] + split3(lse[:, h:h + 1] * (1.0 / SCALE)) + [pad_k], axis=1)
        va = jnp.concatenate([v, minus, pad_v], axis=1)
        da = jnp.concatenate([do] + split3(inner) + [pad_v], axis=1)
        kt = k.astype(f32).T.astype(bf16)
        total = jnp.zeros((HEAD_DIM, count), f32)
        kg, vg = [], []
        for b in range(count // block):
            r = slice(b * block, (b + 1) * block)
            probs = jnp.exp2(mm(ka[r], qa, NT) * factor)
            grad_scores = (probs * mm(va[r], da, NT)).astype(bf16)
            vg.append(mm(probs.astype(bf16), do))
            kg.append(mm(grad_scores, q))
            total = total + mm(kt[:, r], grad_scores)
        key_grads.append(jnp.concatenate(kg, axis=0) * SCALE)
        value_grads.append(jnp.concatenate(vg, axis=0))
        qt_ref[p, :] = total * SCALE
    query_grad = qt_ref[...].T.astype(bf16)
    value_grad = jnp.concatenate(value_grads, axis=1).astype(bf16)
    key_grad = jnp.concatenate(key_grads, axis=1).astype(bf16)
    full = jnp.concatenate([query_grad, key_grad, value_grad], axis=1)
    gn_ref[...] = full[:rows]
    gf_ref[...] = full[rows:]
    sum_ref[0:1, :] = jnp.sum(query_grad.astype(f32), axis=0, keepdims=True)
    sum_ref[1:2, :] = jnp.sum(value_grad.astype(f32), axis=0, keepdims=True)


def attend_back(order, pn, pf, grads, outs, ln, lf, mark_q, mark_k, **more):
    rows = pn.shape[0]
    cols = pn.shape[1] // 3
    count = 2 * rows
    return call(
        order, functools.partial(attend_back_kernel, block=rows),
        [shape((rows, 3 * cols), bf16)] * 2 + [Far(shape((2, cols), f32))],
        [Far(pn), Far(pf)] + list(grads) + [Far(x) for x in list(outs) + [ln, lf, mark_q, mark_k]], "attend_back",
        20 * count * count * cols, scratch=[pltpu.VMEM((cols, count), f32)], limit=14, **more)


def out_kernel(h, vec, a0, w0, a1, w1, a2, w2, a3, w3, res_ref, n_ref):
    total = mm(a1[...], w1[...]) + mm(a2[...], w2[...]) + mm(a3[...], w3[...])
    total = total + mm(a0[...], w0[...]) + h[...].astype(f32) + vec[OUT_BIAS:OUT_BIAS + 1, :]
    res_ref[...] = total
    leave(res_ref)
    unit, _ = unit_of(total)
    n_ref[...] = (unit * vec[GAIN2:GAIN2 + 1, :] + vec[SHIFT2:SHIFT2 + 1, :]).astype(bf16)


def out_project(order, h, vec, atts, ws, **more):
    rows, width = h.shape
    pairs = [Far(atts[0]), ws[0]]
    for a, w in zip(atts[1:], ws[1:]):
        pairs += [a, w]
    return call(
        order, out_kernel, [Far(shape((rows, width), f32)), shape((rows, width), bf16)],
        [Far(h), Far(vec)] + pairs, "out_project", 2 * rows * width * width, **more)


def gelu_both(pre):
    square = pre * pre
    tanh = jnp.tanh(GELU_A * pre * (1.0 + GELU_B * square))
    half = 0.5 * (1.0 + tanh)
    slope = half + 0.5 * pre * (1.0 - tanh * tanh) * (GELU_A * (1.0 + 3.0 * GELU_B * square))
    return pre * half, slope


def grad_act_kernel(ca, cb, w, out):
    rows = ca.shape[0]
    out[:rows] = mm(ca[...], w[...], NT)
    out[rows:] = mm(cb[...], w[...], NT)


def grad_act_of(order, ca, cb, w, **more):
    rows, width = ca.shape
    return call(order, grad_act_kernel, [shape((2 * rows, w.shape[0]), f32)], [ca, cb, w], "grad_act",
                4 * rows * width * w.shape[0], **more)[0]


def hidden_kernel(na, nb, ga, w, vec, act_ref, pre_ref, keep_ref, send_ref, sum_ref):
    rows = na.shape[0]
    sums = jnp.zeros(sum_ref.shape, f32)
    for i, n in enumerate((na, nb)):
        r = slice(i * rows, (i + 1) * rows)
        pre = mm(n[...], w[...], NT) + vec[UP_BIAS:UP_BIAS + 1, :w.shape[0]]
        act, slope = gelu_both(pre)
        act_ref[r] = act.astype(bf16)
        grad = (ga[r] * slope).astype(bf16)
        pre_ref[r] = grad
        sums = sums + jnp.sum(grad.astype(f32), axis=0, keepdims=True)
    sum_ref[...] = sums
    keep_ref[...] = mm(pre_ref[:rows], w[...])
    leave(keep_ref)
    send_ref[...] = mm(pre_ref[rows:], w[...]).astype(bf16)


def hidden(order, na, nb, ga, w, vec, far_keep, **more):
    rows, width = na.shape
    units = w.shape[0]
    keep = shape((rows, width), f32)
    return call(
        order, hidden_kernel,
        [shape((2 * rows, units), bf16)] * 2
        + [Far(keep) if far_keep else keep, shape((rows, width), bf16), Far(shape((1, units), f32))],
        [na, nb, ga, w, Far(vec)], "hidden", 8 * rows * width * units, **more)


def down_kernel(act, w, keep_ref, send_ref):
    rows = keep_ref.shape[0]
    keep_ref[...] = mm(act[:rows], w[...])
    leave(keep_ref)
    send_ref[...] = mm(act[rows:], w[...]).astype(bf16)


def down(order, act, w, far_keep, **more):
    rows, units = act.shape
    width = w.shape[1]
    keep = shape((rows // 2, width), f32)
    return call(order, down_kernel, [Far(keep) if far_keep else keep, shape((rows // 2, width), bf16)], [act, w],
                "down", 2 * rows * width * units, **more)


def insert_bit(j, bit, value):
    low = bit - 1
    return (j // bit) * (2 * bit) + value * bit + (j & low)


SMALL = 16
TOP_ROW = 9
CHUNK = 384


def put_small(ref, base, small):
    for c in range(small.shape[1] // CHUNK):
        part = small[:, c * CHUNK:(c + 1) * CHUNK]
        high = part.astype(bf16)
        at = base + 2 * SMALL * c
        ref[at:at + SMALL, :CHUNK] = high
        ref[at + SMALL:at + 2 * SMALL, :CHUNK] = (part - high.astype(f32)).astype(bf16)


def add_small(small, ref, base):
    parts = []
    for c in range(small.shape[1] // CHUNK):
        at = base + 2 * SMALL * c
        parts.append(ref[at:at + SMALL, :CHUNK].astype(f32) + ref[at + SMALL:at + 2 * SMALL, :CHUNK].astype(f32))
    other = jnp.concatenate(parts, axis=1)
    is_top = lax.broadcasted_iota(jnp.int32, small.shape, 0) == TOP_ROW
    return jnp.where(is_top, jnp.maximum(small, other), small + other)


def weight_small_kernel(mine_ref, xn, xf, gn, gf, sn, sf, sb, un, uf, qv, tn, tf,
                        keep_ref, send_ref, small_ref, lt_ref, acc_ref, *, first, stop, bit):
    kept, block, cols = keep_ref.shape
    rows = xn.shape[0]
    lt_ref[:, :rows] = xn[...].T
    lt_ref[:, rows:] = xf[...].T
    acc_ref[...] = mm(lt_ref[...], jnp.concatenate([gn[:, first:stop], gf[:, first:stop]], axis=0))
    mine = mine_ref[0]
    for j in range(kept):
        at = pl.multiple_of(insert_bit(j, bit, mine) * block, block)
        keep_ref[j] = acc_ref[pl.ds(at, block), :].astype(bf16)
        at = pl.multiple_of(insert_bit(j, bit, 1 - mine) * block, block)
        send_ref[j * block:(j + 1) * block, :] = acc_ref[pl.ds(at, block), :].astype(bf16)
    small_ref[...] = jnp.zeros(small_ref.shape, f32)
    small_ref[0:2, :] = sn[...] + sf[...]
    small_ref[2:6, :] = sb[...]
    small_ref[6:7, :un.shape[1]] = un[...] + uf[...]
    small_ref[7:9, :qv.shape[1]] = qv[...]
    small_ref[TOP_ROW:TOP_ROW + 1, :tn.shape[1]] = jnp.maximum(tn[...], tf[...])
    put_small(send_ref, kept * block, small_ref[...])


def weight_small(order, lefts, rights, smalls, first, stop, mine, bit, parts, name, **more):
    rows, width = lefts[0].shape
    block, cols = width // parts, stop - first
    extra = width // CHUNK * 2 * SMALL
    return call(
        order, functools.partial(weight_small_kernel, first=first, stop=stop, bit=bit),
        [shape((parts // 2, block, cols), bf16), shape((parts // 2 * block + extra, cols), bf16),
         shape((SMALL, width), f32)],
        [mine] + list(lefts) + list(rights) + [Far(x) for x in smalls], name, 4 * width * rows * cols,
        scratch=[pltpu.VMEM((width, 2 * rows), bf16), pltpu.VMEM((width, cols), f32)], smem=1, **more)


def fold_small_kernel(mine_ref, keep_ref, got_ref, small_ref, nk_ref, ns_ref, new_ref, *, bit):
    mine = mine_ref[0]
    parts, block, cols = keep_ref.shape
    kept = nk_ref.shape[0]
    for j in range(kept):
        for side in (0, 1):
            at = insert_bit(j, bit, mine if side == 0 else 1 - mine)
            start = pl.multiple_of(at * block, block)
            total = (keep_ref[at].astype(f32) + got_ref[pl.ds(start, block), :].astype(f32)).astype(bf16)
            if side == 0:
                nk_ref[j] = total
            else:
                ns_ref[j * block:(j + 1) * block, :] = total
    new_ref[...] = add_small(small_ref[...], got_ref, parts * block)
    put_small(ns_ref, kept * block, new_ref[...])


def fold_small(order, keep, got, small, mine, bit, **more):
    parts, block, cols = keep.shape
    extra = got.shape[0] - parts * block
    return call(
        order, functools.partial(fold_small_kernel, bit=bit),
        [shape((parts // 2, block, cols), bf16), shape((parts // 2 * block + extra, cols), bf16),
         shape(small.shape, f32)], [mine, keep, got, small], "fold_small", 2 * keep.size, smem=1, **more)


def weight_kernel(mine_ref, *refs, groups, bit, tile):
    keep_ref, send_ref, lt_ref, acc_ref = refs[-4:]
    kept, block, cols = keep_ref.shape
    products = []
    at = 0
    for lefts, rights, first, stop in groups:
        start = 0
        for x in refs[at:at + lefts]:
            n = x.shape[0]
            lt_ref[:, start:start + n] = x[...].T
            start += n
        at += lefts
        right = [x[:, first:stop] for x in refs[at:at + rights]]
        at += rights
        right = jnp.concatenate(right, axis=0) if rights > 1 else right[0]
        if len(groups) > 1:
            products.append(mm(lt_ref[...], right))
    mine = mine_ref[0]
    for c0 in range(0, cols, tile):
        c1 = min(cols, c0 + tile)
        if products:
            acc_ref[:, :c1 - c0] = jnp.concatenate(products, axis=1)
        else:
            acc_ref[:, :c1 - c0] = mm(lt_ref[...], right[:, c0:c1])
        for j in range(kept):
            for ref, side in ((keep_ref, mine), (send_ref, 1 - mine)):
                row_at = pl.multiple_of(insert_bit(j, bit, side) * block, block)
                ref[j, :, c0:c1] = acc_ref[pl.ds(row_at, block), :c1 - c0].astype(bf16)


def weight_grad(order, groups, mine, bit, parts, name, tile=384, **more):
    width = groups[0][0][0].shape[1]
    count = sum(x.shape[0] for x in groups[0][0])
    cols = sum(stop - first for _, _, first, stop in groups)
    block = width // parts
    if len(groups) > 1:
        tile = cols
    ins = [mine]
    for lefts, rights, _, _ in groups:
        ins += list(lefts) + list(rights)
    sizes = tuple((len(lefts), len(rights), first, stop) for lefts, rights, first, stop in groups)
    return call(
        order, functools.partial(weight_kernel, groups=sizes, bit=bit, tile=tile),
        [shape((parts // 2, block, cols), bf16)] * 2, ins, name, 2 * width * count * cols,
        scratch=[pltpu.VMEM((width, count), bf16), pltpu.VMEM((width, min(tile, cols)), f32)], smem=1, **more)


def fold_kernel(mine_ref, keep_ref, got_ref, nk_ref, ns_ref, *, bit):
    mine = mine_ref[0]
    for j in range(nk_ref.shape[0]):
        for ref, side in ((nk_ref, mine), (ns_ref, 1 - mine)):
            at = insert_bit(j, bit, side)
            ref[j] = (keep_ref[at].astype(f32) + got_ref[at].astype(f32)).astype(bf16)


def fold(order, keep, got, mine, bit, **more):
    parts, block, cols = keep.shape
    return call(order, functools.partial(fold_kernel, bit=bit), [shape((parts // 2, block, cols), bf16)] * 2,
                [mine, keep, got], "fold", 2 * keep.size, smem=1, **more)


def tick_kernel():
    pass


def tick(order, waits):
    call(order, tick_kernel, [], [], "tick", 2e11, waits=waits)


def join_kernel(a, b, out):
    out[...] = (a[...] + b[...].astype(f32)).astype(bf16)


def join(order, a, b, **more):
    return call(order, join_kernel, [shape(a.shape, bf16)], [a, b], "join", a.size, **more)[0]


def finish_kernel(keep_ref, got_ref, out_ref):
    out_ref[...] = keep_ref[0].astype(f32) + got_ref[0].astype(f32)


def finish(order, keep, got, **more):
    return call(order, finish_kernel, [shape(keep.shape[1:], f32)], [keep, got], "finish", keep.size, **more)[0]


def split_kernel(ka, ga, small, kb, gb, qkv_ref, out_ref, new_ref):
    block = ka.shape[1]
    new_ref[...] = add_small(small[...], ga, block)
    whole = jnp.concatenate(
        [ka[0].astype(f32) + ga[:block, :].astype(f32), kb[0].astype(f32) + gb[0].astype(f32)], axis=1)
    cols = out_ref.shape[1]
    for i in range(3):
        qkv_ref[i] = whole[:, i * cols:(i + 1) * cols]
    out_ref[...] = whole[:, 3 * cols:]


def finish_split(order, ka, ga, small, kb, gb, cols, **more):
    rows = ka.shape[1]
    return call(
        order, split_kernel,
        [shape((3, rows, cols), f32), shape((rows, cols), f32), shape(small.shape, f32)],
        [ka, ga, small, kb, gb], "finish_split", ka.size, **more)


def mid_kernel(res, cot, vec, g0, r1, ry, w0, w1, w2, w3, gr_ref, gb_ref, a0, a1, a2, a3, sum_ref):
    unit, inverse = unit_of(res[...])
    top = cot[...].astype(f32)
    grad = g0[...] + r1[...].astype(f32) + ry[...].astype(f32)
    resid = top + norm_back(grad, unit, inverse, vec[GAIN2:GAIN2 + 1, :])
    gr_ref[...] = resid
    leave(gr_ref)
    branch = resid.astype(bf16)
    gb_ref[...] = branch
    for a, w in ((a2, w2), (a3, w3), (a1, w1), (a0, w0)):
        a[...] = mm(branch, w[...], NT).astype(bf16)
    for i, x in enumerate((resid, grad * unit, grad, top)):
        sum_ref[i:i + 1, :] = jnp.sum(x, axis=0, keepdims=True)


def mid(order, res, cot, vec, g0, r1, ry, ws, **more):
    rows, width = g0.shape
    cols = ws[0].shape[0]
    return call(
        order, mid_kernel,
        [Far(shape((rows, width), f32)), shape((rows, width), bf16)] + [shape((rows, cols), bf16)] * 4
        + [Far(shape((4, width), f32))],
        [Far(res), Far(cot), Far(vec), Far(g0), r1, ry] + list(ws), "mid", 2 * rows * width * width, **more)


def grad_norm_kernel(g, w, xa, xb, keep_ref, send_ref, sum_ref):
    rows = xa.shape[0]
    sums = [0.0, 0.0]
    for i, (x, ref) in enumerate(((xa, keep_ref), (xb, send_ref))):
        r = slice(i * rows, (i + 1) * rows)
        grad = mm(g[r], w[...])
        ref[...] = grad.astype(ref.dtype)
        leave(ref)
        unit, _ = unit_of(x[...].astype(f32))
        sums[0] = sums[0] + jnp.sum(grad * unit, axis=0, keepdims=True)
        sums[1] = sums[1] + jnp.sum(grad, axis=0, keepdims=True)
    sum_ref[0:1, :] = sums[0]
    sum_ref[1:2, :] = sums[1]


def grad_norm(order, g, w, xa, xb, far_keep, **more):
    rows, width = xa.shape
    keep = shape((rows, width), f32)
    return call(
        order, grad_norm_kernel,
        [Far(keep) if far_keep else keep, shape((rows, width), bf16), Far(shape((2, width), f32))],
        [g, w, Far(xa), Far(xb)], "grad_norm", 4 * rows * width * g.shape[1], **more)


def last_kernel(x, gr, vec, g0, r1, ry, out):
    unit, inverse = unit_of(x[...].astype(f32))
    grad = g0[...] + r1[...].astype(f32) + ry[...].astype(f32)
    out[...] = (gr[...] + norm_back(grad, unit, inverse, vec[GAIN1:GAIN1 + 1, :])).astype(bf16)


def last(order, x, gr, vec, g0, r1, ry, **more):
    return call(order, last_kernel, [Far(shape(x.shape, bf16))], [Far(x), Far(gr), Far(vec), Far(g0), r1, ry], "last",
                20 * x.size, **more)[0]


def make_local(dp_size, tensor_size):
    def scatter_plain(groups):
        index = lax.axis_index("dp")
        value = jnp.concatenate(
            [mm(jnp.concatenate(lefts), jnp.concatenate([x[:, first:stop] for x in rights]), TN)
             for lefts, rights, first, stop in groups], axis=1).astype(bf16)
        width, cols = value.shape
        block = width // dp_size
        bit = 1
        while bit < dp_size:
            count = value.shape[0] // block // 2
            pairs = value.reshape(count, 2, block, cols)
            mine = (index // bit) % 2
            keep = lax.dynamic_index_in_dim(pairs, mine, 1, keepdims=False)
            send = lax.dynamic_index_in_dim(pairs, 1 - mine, 1, keepdims=False)
            value = keep.astype(f32) + swap(send, "dp", dp_size, bit).astype(f32)
            bit *= 2
            if bit < dp_size:
                value = value.astype(bf16)
            value = value.reshape(count * block, cols)
        return value

    class Spread:
        def __init__(self, order, groups, bits, name, **more):
            width = groups[0][0][0].shape[1]
            self.order, self.bits, self.index = order, bits, lax.axis_index("dp")
            self.paired = dp_size == 8 and (width // dp_size) % 16 == 0
            if self.paired:
                self.step = 0
                self.keep, send = weight_grad(order, groups, self.mine(bits[0]), bits[0], dp_size, name, **more)
                self.got = swap(after(send, order.last), "dp", dp_size, bits[0])
            else:
                self.value = scatter_plain(groups)

        def mine(self, bit):
            return ((self.index // bit) % 2).astype(jnp.int32).reshape(1)

        def local_bit(self):
            bit = local = self.bits[self.step]
            for used in self.bits[:self.step]:
                if used < bit:
                    local //= 2
            return bit, local

        def fold(self, **more):
            if self.paired:
                self.step += 1
                bit, local_bit = self.local_bit()
                self.keep, send = fold(self.order, self.keep, self.got, self.mine(bit), local_bit, **more)
                self.got = swap(after(send, self.order.last), "dp", dp_size, bit)

        def result(self, **more):
            if self.paired:
                return finish(self.order, self.keep, self.got, **more)
            return self.value

    class SpreadSmall(Spread):
        def __init__(self, order, lefts, rights, smalls, first, stop, bits, name, **more):
            width = lefts[0].shape[1]
            self.order, self.bits, self.index, self.step = order, bits, lax.axis_index("dp"), 0
            self.keep, send, self.small = weight_small(
                order, lefts, rights, smalls, first, stop, self.mine(bits[0]), bits[0], dp_size, name, **more)
            self.got = swap(after(send, order.last), "dp", dp_size, bits[0])

        def fold(self, **more):
            self.step += 1
            bit, local_bit = self.local_bit()
            self.keep, send, self.small = fold_small(
                self.order, self.keep, self.got, self.small, self.mine(bit), local_bit, **more)
            self.got = swap(after(send, self.order.last), "dp", dp_size, bit)

    def local(hidden_in, picture_ids, norm1_gain, norm1_bias, w_qkv, qv_bias, w_out, out_bias,
              norm2_gain, norm2_bias, w_up, up_bias, w_down, down_bias, cotangent):
        rows, width = hidden_in.shape
        head_width = w_qkv.shape[2]
        place = lax.axis_index("tensor")
        order = Order()
        units = w_up.shape[1]
        wt_qkv = w_qkv.transpose(0, 2, 1).reshape(3 * head_width, width)
        wt_up = w_up.T
        index = lax.axis_index("dp")

        def pin(value):
            return value if order.last is None else after(value, order.last)

        def core(value):
            return swap(pin(value), "tensor", tensor_size, 1)

        def across(value):
            return swap(pin(value), "tensor", tensor_size, 2)

        def diagonal(value):
            return swap(pin(value), "tensor", tensor_size, 3)

        def double(value, bit):
            other = swap(pin(value), "dp", dp_size, bit)
            low = (index // bit) % 2 == 0
            return jnp.concatenate([jnp.where(low, value, other), jnp.where(low, other, value)])

        paired = dp_size == 8 and (width // dp_size) % 16 == 0
        h2 = across(hidden_in)
        h1, c1, w1 = core(hidden_in), core(cotangent), core(w_out)
        mark_q, mark_k, vec = marks(
            order, place.astype(jnp.int32).reshape(1), picture_ids.reshape(tensor_size, rows),
            [norm1_gain, norm1_bias, norm2_gain, norm2_bias, out_bias, up_bias, qv_bias, down_bias])
        nn, pn, pn_far = qkv(order, hidden_in, h1, vec, wt_qkv)
        h3 = core(h2)
        w2 = across(after(w_out, h2))
        nf, pf, pf_far = qkv(order, h2, h3, vec, wt_qkv, waits=[c1])
        a2, a3, lse_f, top_f = attend(order, pf, pn, pf, mark_q, mark_k, 2 * rows, waits=[w1])
        got2, got3 = across(a2), diagonal(a3)
        a0, a1, lse_n, top_n = attend(order, pn, pn, pf, mark_q, mark_k, 0)
        got1, w3 = core(a1), core(w2)
        c2 = across(cotangent)
        ga_n = grad_act_of(order, cotangent, c1, w_down)
        tick(order, [got2, got3])
        ws = [w_out, w1, w2, w3]
        residual, normed_b = out_project(order, hidden_in, vec, [a0, got1, got2, got3], ws)
        b2, b1 = across(normed_b), core(normed_b)
        c3 = core(c2)
        act_n, pre_n, g0, g1, up_n = hidden(order, normed_b, b1, ga_n, wt_up, vec, True)
        b3, r1 = core(b2), core(g1)
        ga_f = grad_act_of(order, c2, c3, w_down)
        act_f, pre_f, g2, g3, up_f = hidden(order, b2, b3, ga_f, wt_up, vec, False)
        r3 = core(g3)
        m0, m1 = down(order, act_n, w_down, True, waits=[r1])
        n1 = core(m1)
        ry = across(join(order, g2, r3))
        s_up = Spread(order, [([normed_b, b1, b2, b3], [pre_n, pre_f], 0, units)], (1, 2, 4), "weight_up")
        s_down = Spread(order, [([cotangent, c1, c2, c3], [act_n, act_f], 0, units)], (1, 2, 4), "weight_down",
                        waits=[n1])
        grad_resid, branch, p0, p1, p2, p3, sums_b = mid(order, residual, cotangent, vec, g0, r1, ry, ws)
        d = [p0, core(p1), across(p2), diagonal(p3)]
        m2, m3 = down(order, act_f, w_down, False)
        n3 = core(m3)
        s_up.fold()
        n2 = join(order, m2, n3)
        gb2 = across(after(branch, d[2], d[3]))
        gq_n, gq_f, sums_qv = attend_back(
            order, pn_far, pf_far, d, [a0, a1, a2, a3], lse_n, lse_f, mark_q, mark_k)
        gb3, gb1 = core(gb2), core(branch)
        s_up.fold()
        e2, e3, sums_f = grad_norm(order, gq_f, wt_qkv, h2, h3, False)
        f3 = core(e3)
        cut = 512 if paired else head_width
        s_down.fold()
        s_vo = Spread(order, [([nn, nf], [gq_n, gq_f], cut, 3 * head_width),
                              ([branch, gb1, gb2, gb3], [a0, a1, a2, a3], 0, head_width)], (1, 2, 4), "weight_vo")
        fy = across(join(order, e2, f3))
        e0, e1, sums_n = grad_norm(order, gq_n, wt_qkv, hidden_in, h1, True)
        f1 = core(e1)
        smalls = [sums_n, sums_f, sums_b, up_n, up_f, sums_qv, top_n, top_f]
        if paired:
            s_qk = SpreadSmall(order, [nn, nf], [gq_n, gq_f], smalls, 0, cut, (2, 1, 4), "weight_qk")
        else:
            s_qk = Spread(order, [([nn, nf], [gq_n, gq_f], 0, cut)], (2, 1, 4), "weight_qk")
        g_up = s_up.result()
        s_down.fold()
        ny = across(after(n2, fy))
        s_vo.fold()
        grad_in = last(order, hidden_in, grad_resid, vec, e0, f1, fy)
        s_qk.fold()
        s_vo.fold()
        g_down = s_down.result()
        s_qk.fold()
        hidden_out = (residual + m0 + n1.astype(f32) + ny.astype(f32) + down_bias).astype(bf16)
        if paired:
            g_qkv, g_out, small = finish_split(order, s_qk.keep, s_qk.got, s_qk.small, s_vo.keep, s_vo.got, head_width,
                                               waits=[hidden_out])
        else:
            last_w = jnp.concatenate([s_qk.result(), s_vo.result()], axis=1)
            g_qkv = jnp.stack([last_w[:, i * head_width:(i + 1) * head_width] for i in range(3)])
            g_out = last_w[:, 3 * head_width:]
            wide = lambda x: jnp.pad(x, ((0, 0), (0, width - x.shape[1])))
            small = jnp.concatenate([sums_n + sums_f, sums_b, wide(up_n + up_f), wide(sums_qv),
                                     wide(jnp.maximum(top_n, top_f))])
            bit = 1
            while bit < dp_size:
                other = swap(small, "dp", dp_size, bit)
                small = jnp.concatenate([small[:TOP_ROW] + other[:TOP_ROW], jnp.maximum(small[TOP_ROW:], other[TOP_ROW:])])
                bit *= 2
        shared = small[:8]
        shared = shared + swap(shared, "tensor", tensor_size, 1)
        shared = shared + swap(shared, "tensor", tensor_size, 2)
        top = small[TOP_ROW, :head_width // HEAD_DIM]
        limit = jnp.float32(CLIP_LIMIT)
        factor = jnp.sqrt(limit / jnp.maximum(top, limit))
        column = jnp.repeat(factor, HEAD_DIM)
        scaled_qk = (w_qkv[:2].astype(f32) * column).astype(bf16)
        scaled_query_bias = qv_bias[0] * column
        return (hidden_out, grad_in, g_qkv, g_out.T, g_up, g_down.T, small[7:9, :head_width], small[6, :units],
                shared[:6], top, scaled_qk, scaled_query_bias)

    return local


def solution(mesh):
    return jax.shard_map(
        make_local(mesh.shape["dp"], mesh.shape["tensor"]),
        mesh=mesh,
        in_specs=(
            P(("dp", "tensor"), None), P("dp"), P(), P(), P(None, None, "tensor"), P(None, "tensor"),
            P("tensor", None), P(), P(), P(), P(None, "tensor"), P("tensor"), P("tensor", None), P(),
            P(("dp", "tensor"), None),
        ),
        out_specs=(
            P(("dp", "tensor"), None), P(("dp", "tensor"), None), P(None, "dp", "tensor"), P("tensor", "dp"),
            P("dp", "tensor"), P("tensor", "dp"), P(None, "tensor"), P("tensor"), P(), P("tensor"),
            P(None, None, "tensor"), P("tensor"),
        ),
        check_vma=False,
    )
```

```python
import functools
import math

import jax
import jax.numpy as jnp
from jax import lax
from jax.experimental import pallas as pl
from jax.experimental.pallas import tpu as pltpu
from jax.sharding import PartitionSpec as P

HEAD_DIM = 72
PACK = 1024
CLIP_LIMIT = 9
LANES = 128
SPARE = LANES - HEAD_DIM
SCALE = HEAD_DIM ** (-0.5)
LOG2E = 1.4426950408889634
GELU_A = 0.7978845608028654
GELU_B = 0.044715

eps_norm = 1e-06
neg_fill = -1e30
f32 = jnp.float32
bf16 = jnp.bfloat16
NN = (((1,), (0,)), ((), ()))
NT = (((1,), (1,)), ((), ()))
TN = (((0,), (0,)), ((), ()))


def mm(left, right, dims=NN):
    return lax.dot_general(left, right, dims, preferred_element_type=f32)


def swap(value, axis, size, bit):
    return lax.ppermute(value, axis, [(i, i ^ bit) for i in range(size)])


def after(value, *others):
    return lax.optimization_barrier((value,) + others)[0]


class Far:
    def __init__(self, value):
        self.value = value


class Lazy:
    def __init__(self, ref, copy):
        self.ref, self.copy, self.shape, self.dtype = ref, copy, ref.shape, ref.dtype

    def __getitem__(self, index):
        if self.copy is not None:
            self.copy.wait()
            self.copy = None
        return self.ref[index]


class Out:
    def __init__(self, ref, copy):
        self.ref, self.copy, self.shape, self.dtype, self.left = ref, copy, ref.shape, ref.dtype, False

    def __getitem__(self, index):
        return self.ref[index]

    def __setitem__(self, index, value):
        self.ref[index] = value

    def leave(self):
        if not self.left:
            self.copy.start()
            self.left = True


def leave(ref):
    if isinstance(ref, Out):
        ref.leave()


class Order:
    def __init__(self):
        self.last = None


def call(order, kernel, outs, ins, name, flops, scratch=(), limit=9, smem=0, waits=()):
    near = pl.BlockSpec(memory_space=pltpu.VMEM)
    far = pl.BlockSpec(memory_space=pltpu.HBM)
    scalar = pl.BlockSpec(memory_space=pltpu.SMEM)
    in_far = [isinstance(x, Far) for x in ins]
    out_far = [isinstance(x, Far) for x in outs]
    ins = [x.value if isinstance(x, Far) else x for x in ins]
    outs = [x.value if isinstance(x, Far) else x for x in outs]
    moved = sum(x.size * x.dtype.itemsize for x in outs + ins)
    unread = ([] if order.last is None else [order.last]) + list(waits)
    count, extra = len(ins), len(scratch)
    buffers = [pltpu.VMEM(x.shape, x.dtype) for x, f in zip(ins + outs, in_far + out_far) if f]

    def body(*refs):
        in_refs, refs = refs[:count], refs[count + len(unread):]
        out_refs, refs = refs[:len(outs)], refs[len(outs) + 1:]
        own, refs = refs[:extra], refs[extra:]
        buffer_refs, sems = list(refs[:len(buffers)]), refs[len(buffers):]
        slot = 0
        given, leaving = [], []
        for ref, f in zip(in_refs, in_far):
            if f:
                copy = pltpu.make_async_copy(ref, buffer_refs[slot], sems[0].at[slot])
                copy.start()
                ref = Lazy(buffer_refs[slot], copy)
                slot += 1
            given.append(ref)
        for ref, f in zip(out_refs, out_far):
            if f:
                ref = Out(buffer_refs[slot], pltpu.make_async_copy(buffer_refs[slot], ref, sems[0].at[slot]))
                leaving.append(ref)
                slot += 1
            given.append(ref)
        kernel(*given, *own)
        for ref in given:
            if isinstance(ref, Lazy) and ref.copy is not None:
                ref.copy.wait()
        for ref in leaving:
            ref.leave()
        for ref in leaving:
            ref.copy.wait()

    size = sum(math.prod(x.shape) * x.dtype.itemsize for x, f in zip(ins + outs, in_far + out_far) if f)
    results = pl.pallas_call(
        body,
        out_shape=tuple(pltpu.HBM(x.shape, x.dtype) if f else x for x, f in zip(outs, out_far))
        + (pltpu.HBM((8, LANES), f32),),
        in_specs=[scalar] * smem + [far if f else near for f in in_far[smem:]] + [pl.BlockSpec(memory_space=pl.ANY)] * len(unread),
        out_specs=tuple(far if f else near for f in out_far) + (far,),
        scratch_shapes=list(scratch) + buffers + ([pltpu.SemaphoreType.DMA((len(buffers),))] if buffers else []),
        compiler_params=pltpu.CompilerParams(vmem_limit_bytes=limit * 2**20 + size + size // 4),
        cost_estimate=pl.CostEstimate(flops=int(flops), bytes_accessed=int(moved), transcendentals=0),
        name=name,
    )(*(pltpu.with_memory_space_constraint(x, pltpu.HBM) if f else x for x, f in zip(ins, in_far)), *(pltpu.with_memory_space_constraint(x, pltpu.HBM) if i == 0 and order.last is not None else x
                                                                              for i, x in enumerate(unread)))
    order.last = results[-1]
    return results[:-1]


def shape(dims, dtype):
    return jax.ShapeDtypeStruct(tuple(dims), dtype)


def row(vector):
    return vector.reshape(1, -1)


def unit_of(values_in):
    row_mean = jnp.mean(values_in, axis=-1, keepdims=True)
    centred = values_in - row_mean
    variance = jnp.mean(centred * centred, axis=-1, keepdims=True)
    inverse = lax.rsqrt(variance + eps_norm)
    return centred * inverse, inverse


def norm_back(grad_rows, unit_rows, inverse, gain):
    scaled = grad_rows * gain
    return inverse * (
        scaled
        - jnp.mean(scaled, axis=-1, keepdims=True)
        - unit_rows * jnp.mean(scaled * unit_rows, axis=-1, keepdims=True)
    )


GAIN1, SHIFT1, GAIN2, SHIFT2, OUT_BIAS, UP_BIAS, QKV_BIAS, DOWN_BIAS = range(8)


def qkv_kernel(vec, xa, xb, w, n_ref, p_ref, copy_ref):
    rows = xa.shape[0]
    cols = w.shape[0]
    for i, x in enumerate((xa, xb)):
        unit, _ = unit_of(x[...].astype(f32))
        n_ref[i * rows:(i + 1) * rows, :] = (
            unit * vec[GAIN1:GAIN1 + 1, :] + vec[SHIFT1:SHIFT1 + 1, :]).astype(bf16)
    leave(n_ref)
    p_ref[...] = (mm(n_ref[...], w[...], NT) + vec[QKV_BIAS:QKV_BIAS + 1, :cols]).astype(bf16)
    copy_ref[...] = p_ref[...]


def qkv(order, xa, xb, vec, w, **more):
    rows, width = xa.shape
    cols = w.shape[0]
    return call(
        order, qkv_kernel,
        [Far(shape((2 * rows, width), bf16)), shape((2 * rows, cols), bf16), Far(shape((2 * rows, cols), bf16))],
        [Far(vec), xa, xb, w], "qkv", 4 * rows * width * cols, **more)


def marks_kernel(place_ref, ids_ref, g1, s1, g2, s2, ob, ub, qv, db, q_ref, k_ref, vec_ref):
    rows = ids_ref.shape[1]
    lane = lax.broadcasted_iota(jnp.int32, (LANES, rows), 0)
    for slot in range(ids_ref.shape[0]):
        ids = ids_ref[pl.ds(place_ref[0] ^ slot, 1), :]
        same = jnp.where((ids + 1) == lane, 1.0, 0.0).T[:, :SPARE]
        r = slice(slot * rows, (slot + 1) * rows)
        q_ref[r, :] = same.astype(bf16)
        k_ref[r, :] = jnp.where(same > 0.5, 0.0, neg_fill).astype(bf16)
    for i, x in ((GAIN1, g1), (SHIFT1, s1), (GAIN2, g2), (SHIFT2, s2), (OUT_BIAS, ob), (UP_BIAS, ub), (DOWN_BIAS, db)):
        vec_ref[i:i + 1, :x.shape[0]] = x[...].reshape(1, x.shape[0])
    cols = qv.shape[1]
    biases = jnp.concatenate([qv[0:1, :], jnp.zeros((1, cols), f32), qv[1:2, :]], axis=1)
    vec_ref[QKV_BIAS:QKV_BIAS + 1, :3 * cols] = biases


def marks(order, place, ids, vectors):
    width = vectors[0].shape[0]
    return call(order, marks_kernel,
                [Far(x) for x in [shape((ids.size, SPARE), bf16)] * 2 + [shape((8, width), f32)]],
                [place, ids] + [Far(x) for x in vectors], "marks", ids.size, smem=1)


def attend_kernel(p_ref, kn, kf, mark_q, mark_k, oa_ref, ob_ref, lse_ref, top_ref, *, block, first):
    rows = p_ref.shape[0]
    cols = oa_ref.shape[1]
    heads = cols // HEAD_DIM
    factor = SCALE * LOG2E
    keys = jnp.concatenate([kn[:, cols:], kf[:, cols:]], axis=0)
    marked = mark_k[...]
    ones = jnp.where(lax.broadcasted_iota(jnp.int32, marked.shape, 1) == 0, 1.0, 0.0).astype(bf16)
    parts = [slice(h * HEAD_DIM, (h + 1) * HEAD_DIM) for h in range(heads)]
    ka = [jnp.concatenate([keys[:, p], marked], axis=1) for p in parts]
    va = [jnp.concatenate([keys[:, cols + p.start:cols + p.stop], ones], axis=1) for p in parts]
    qa = [jnp.concatenate([p_ref[:, p], mark_q[first:first + rows, :]], axis=1) for p in parts]
    blocks = rows // block
    steps = [(h, b) for h in range(heads) for b in range(blocks)]

    def score(i):
        h, b = steps[i]
        return mm(qa[h][b * block:(b + 1) * block], ka[h], NT)

    outs, lses, tops = {}, {}, {}
    ahead = score(0)
    for i, (h, b) in enumerate(steps):
        scores = ahead
        if i + 1 < len(steps):
            ahead = score(i + 1)
        top = jnp.max(scores, axis=1, keepdims=True)
        probs = jnp.exp2(scores * factor - top * factor).astype(bf16)
        out = mm(probs, va[h])
        total = out[:, HEAD_DIM:HEAD_DIM + 1]
        outs[h, b] = out[:, :HEAD_DIM] * (1.0 / total)
        lses[h, b] = top * SCALE + jnp.log(total)
        tops.setdefault(h, []).append(jnp.max(top, axis=0, keepdims=True))
    flat = [jnp.concatenate([outs[h, b] for h in range(heads)], axis=1).astype(bf16) for b in range(blocks)]
    half = blocks // 2
    oa_ref[...] = jnp.concatenate(flat[:half], axis=0)
    ob_ref[...] = jnp.concatenate(flat[half:], axis=0)
    for b in range(blocks):
        lse_ref[b * block:(b + 1) * block, :] = jnp.concatenate([lses[h, b] for h in range(heads)], axis=1)
    top_ref[...] = jnp.concatenate([functools.reduce(jnp.maximum, tops[h]) * SCALE for h in range(heads)], axis=1)


def attend(order, p, pn, pf, mark_q, mark_k, first, **more):
    rows = p.shape[0]
    cols = p.shape[1] // 3
    count = mark_k.shape[0]
    heads = cols // HEAD_DIM
    return call(
        order, functools.partial(attend_kernel, block=rows // 2, first=first),
        [Far(x) for x in [shape((rows // 2, cols), bf16)] * 2 + [shape((rows, heads), f32), shape((1, heads), f32)]],
        [p, pn, pf, Far(mark_q), Far(mark_k)], "attend", 8 * rows * count * cols, **more)


def split3(value):
    high = value.astype(bf16)
    rest = value - high.astype(f32)
    middle = rest.astype(bf16)
    return [high, middle, (rest - middle.astype(f32)).astype(bf16)]


def attend_back_kernel(*refs, block):
    (pn, pf, d0, d1, d2, d3, a0, a1, a2, a3, ln, lf, mq_ref, mk_ref,
     gn_ref, gf_ref, sum_ref, qt_ref) = refs
    rows = pn.shape[0]
    cols = d0.shape[1]
    count = 2 * rows
    heads = cols // HEAD_DIM
    factor = SCALE * LOG2E
    cat = lambda *xs: jnp.concatenate([x[...] for x in xs], axis=0)
    whole = cat(pn, pf)
    queries, keys, values = whole[:, :cols], whole[:, cols:2 * cols], whole[:, 2 * cols:]
    grads, outs, lse = cat(d0, d1, d2, d3), cat(a0, a1, a2, a3), cat(ln, lf)
    mark_q, mark_k = mq_ref[:, :16], mk_ref[:, :16]
    minus = jnp.full((count, 3), -1.0, bf16)
    pad_k = jnp.zeros((count, SPARE - 16 - 3), bf16)
    pad_v = jnp.zeros((count, SPARE - 3), bf16)
    key_grads, value_grads = [], []
    for h in range(heads):
        p = slice(h * HEAD_DIM, (h + 1) * HEAD_DIM)
        k, q, v, do = keys[:, p], queries[:, p], values[:, p], grads[:, p]
        inner = jnp.sum(do.astype(f32) * outs[:, p].astype(f32), axis=1, keepdims=True)
        ka = jnp.concatenate([k, mark_k, minus, pad_k], axis=1)
        qa = jnp.concatenate([q, mark_q] + split3(lse[:, h:h + 1] * (1.0 / SCALE)) + [pad_k], axis=1)
        va = jnp.concatenate([v, minus, pad_v], axis=1)
        da = jnp.concatenate([do] + split3(inner) + [pad_v], axis=1)
        kt = k.astype(f32).T.astype(bf16)
        total = jnp.zeros((HEAD_DIM, count), f32)
        kg, vg = [], []
        for b in range(count // block):
            r = slice(b * block, (b + 1) * block)
            probs = jnp.exp2(mm(ka[r], qa, NT) * factor)
            grad_scores = (probs * mm(va[r], da, NT)).astype(bf16)
            vg.append(mm(probs.astype(bf16), do))
            kg.append(mm(grad_scores, q))
            total = total + mm(kt[:, r], grad_scores)
        key_grads.append(jnp.concatenate(kg, axis=0) * SCALE)
        value_grads.append(jnp.concatenate(vg, axis=0))
        qt_ref[p, :] = total * SCALE
    query_grad = qt_ref[...].T.astype(bf16)
    value_grad = jnp.concatenate(value_grads, axis=1).astype(bf16)
    key_grad = jnp.concatenate(key_grads, axis=1).astype(bf16)
    full = jnp.concatenate([query_grad, key_grad, value_grad], axis=1)
    gn_ref[...] = full[:rows]
    gf_ref[...] = full[rows:]
    sum_ref[0:1, :] = jnp.sum(query_grad.astype(f32), axis=0, keepdims=True)
    sum_ref[1:2, :] = jnp.sum(value_grad.astype(f32), axis=0, keepdims=True)


def attend_back(order, pn, pf, grads, outs, ln, lf, mark_q, mark_k, **more):
    rows = pn.shape[0]
    cols = pn.shape[1] // 3
    count = 2 * rows
    return call(
        order, functools.partial(attend_back_kernel, block=rows),
        [shape((rows, 3 * cols), bf16)] * 2 + [Far(shape((2, cols), f32))],
        [Far(pn), Far(pf)] + list(grads) + [Far(x) for x in list(outs) + [ln, lf, mark_q, mark_k]], "attend_back",
        20 * count * count * cols, scratch=[pltpu.VMEM((cols, count), f32)], limit=14, **more)


def out_kernel(h, vec, a0, w0, a1, w1, a2, w2, a3, w3, res_ref, n_ref):
    total = mm(a1[...], w1[...]) + mm(a2[...], w2[...]) + mm(a3[...], w3[...])
    total = total + mm(a0[...], w0[...]) + h[...].astype(f32) + vec[OUT_BIAS:OUT_BIAS + 1, :]
    res_ref[...] = total
    leave(res_ref)
    unit, _ = unit_of(total)
    n_ref[...] = (unit * vec[GAIN2:GAIN2 + 1, :] + vec[SHIFT2:SHIFT2 + 1, :]).astype(bf16)


def out_project(order, h, vec, atts, ws, **more):
    rows, width = h.shape
    pairs = [Far(atts[0]), ws[0]]
    for a, w in zip(atts[1:], ws[1:]):
        pairs += [a, w]
    return call(
        order, out_kernel, [Far(shape((rows, width), f32)), shape((rows, width), bf16)],
        [Far(h), Far(vec)] + pairs, "out_project", 2 * rows * width * width, **more)


def gelu_both(pre):
    square = pre * pre
    tanh = jnp.tanh(GELU_A * pre * (1.0 + GELU_B * square))
    half = 0.5 * (1.0 + tanh)
    slope = half + 0.5 * pre * (1.0 - tanh * tanh) * (GELU_A * (1.0 + 3.0 * GELU_B * square))
    return pre * half, slope


def grad_act_kernel(ca, cb, w, out):
    rows = ca.shape[0]
    out[:rows] = mm(ca[...], w[...], NT)
    out[rows:] = mm(cb[...], w[...], NT)


def grad_act_of(order, ca, cb, w, **more):
    rows, width = ca.shape
    return call(order, grad_act_kernel, [shape((2 * rows, w.shape[0]), f32)], [ca, cb, w], "grad_act",
                4 * rows * width * w.shape[0], **more)[0]


def hidden_kernel(na, nb, ga, w, vec, act_ref, pre_ref, keep_ref, send_ref, sum_ref):
    rows = na.shape[0]
    sums = jnp.zeros(sum_ref.shape, f32)
    for i, n in enumerate((na, nb)):
        r = slice(i * rows, (i + 1) * rows)
        pre = mm(n[...], w[...], NT) + vec[UP_BIAS:UP_BIAS + 1, :w.shape[0]]
        act, slope = gelu_both(pre)
        act_ref[r] = act.astype(bf16)
        grad = (ga[r] * slope).astype(bf16)
        pre_ref[r] = grad
        sums = sums + jnp.sum(grad.astype(f32), axis=0, keepdims=True)
    sum_ref[...] = sums
    leave(sum_ref)
    keep_ref[...] = mm(pre_ref[:rows], w[...])
    leave(keep_ref)
    send_ref[...] = mm(pre_ref[rows:], w[...]).astype(bf16)


def hidden(order, na, nb, ga, w, vec, far_keep, **more):
    rows, width = na.shape
    units = w.shape[0]
    keep = shape((rows, width), f32)
    return call(
        order, hidden_kernel,
        [shape((2 * rows, units), bf16)] * 2
        + [Far(keep) if far_keep else keep, shape((rows, width), bf16), Far(shape((1, units), f32))],
        [na, nb, ga, w, Far(vec)], "hidden", 8 * rows * width * units, **more)


def down_kernel(act, w, keep_ref, send_ref):
    rows = keep_ref.shape[0]
    keep_ref[...] = mm(act[:rows], w[...])
    leave(keep_ref)
    send_ref[...] = mm(act[rows:], w[...]).astype(bf16)


def down(order, act, w, far_keep, **more):
    rows, units = act.shape
    width = w.shape[1]
    keep = shape((rows // 2, width), f32)
    return call(order, down_kernel, [Far(keep) if far_keep else keep, shape((rows // 2, width), bf16)], [act, w],
                "down", 2 * rows * width * units, **more)


def insert_bit(j, bit, value):
    low = bit - 1
    return (j // bit) * (2 * bit) + value * bit + (j & low)


SMALL = 16
TOP_ROW = 9
CHUNK = 384


def put_small(ref, base, small):
    for c in range(small.shape[1] // CHUNK):
        part = small[:, c * CHUNK:(c + 1) * CHUNK]
        high = part.astype(bf16)
        at = base + 2 * SMALL * c
        ref[at:at + SMALL, :CHUNK] = high
        ref[at + SMALL:at + 2 * SMALL, :CHUNK] = (part - high.astype(f32)).astype(bf16)


def add_small(small, ref, base):
    parts = []
    for c in range(small.shape[1] // CHUNK):
        at = base + 2 * SMALL * c
        parts.append(ref[at:at + SMALL, :CHUNK].astype(f32) + ref[at + SMALL:at + 2 * SMALL, :CHUNK].astype(f32))
    other = jnp.concatenate(parts, axis=1)
    is_top = lax.broadcasted_iota(jnp.int32, small.shape, 0) == TOP_ROW
    return jnp.where(is_top, jnp.maximum(small, other), small + other)


def weight_small_kernel(mine_ref, xn, xf, gn, gf, sn, sf, sb, un, uf, qv, tn, tf,
                        keep_ref, send_ref, small_ref, lt_ref, acc_ref, *, first, stop, bit):
    kept, block, cols = keep_ref.shape
    rows = xn.shape[0]
    lt_ref[:, :rows] = xn[...].T
    lt_ref[:, rows:] = xf[...].T
    acc_ref[...] = mm(lt_ref[...], jnp.concatenate([gn[:, first:stop], gf[:, first:stop]], axis=0))
    mine = mine_ref[0]
    for j in range(kept):
        at = pl.multiple_of(insert_bit(j, bit, mine) * block, block)
        keep_ref[j] = acc_ref[pl.ds(at, block), :].astype(bf16)
        at = pl.multiple_of(insert_bit(j, bit, 1 - mine) * block, block)
        send_ref[j * block:(j + 1) * block, :] = acc_ref[pl.ds(at, block), :].astype(bf16)
    small_ref[...] = jnp.zeros(small_ref.shape, f32)
    small_ref[0:2, :] = sn[...] + sf[...]
    small_ref[2:6, :] = sb[...]
    small_ref[6:7, :un.shape[1]] = un[...] + uf[...]
    small_ref[7:9, :qv.shape[1]] = qv[...]
    small_ref[TOP_ROW:TOP_ROW + 1, :tn.shape[1]] = jnp.maximum(tn[...], tf[...])
    put_small(send_ref, kept * block, small_ref[...])


def weight_small(order, lefts, rights, smalls, first, stop, mine, bit, parts, name, **more):
    rows, width = lefts[0].shape
    block, cols = width // parts, stop - first
    extra = width // CHUNK * 2 * SMALL
    return call(
        order, functools.partial(weight_small_kernel, first=first, stop=stop, bit=bit),
        [shape((parts // 2, block, cols), bf16), shape((parts // 2 * block + extra, cols), bf16),
         shape((SMALL, width), f32)],
        [mine] + list(lefts) + list(rights) + [Far(x) for x in smalls], name, 4 * width * rows * cols,
        scratch=[pltpu.VMEM((width, 2 * rows), bf16), pltpu.VMEM((width, cols), f32)], smem=1, **more)


def fold_small_kernel(mine_ref, keep_ref, got_ref, small_ref, nk_ref, ns_ref, new_ref, *, bit):
    mine = mine_ref[0]
    parts, block, cols = keep_ref.shape
    kept = nk_ref.shape[0]
    for j in range(kept):
        for side in (0, 1):
            at = insert_bit(j, bit, mine if side == 0 else 1 - mine)
            start = pl.multiple_of(at * block, block)
            total = (keep_ref[at].astype(f32) + got_ref[pl.ds(start, block), :].astype(f32)).astype(bf16)
            if side == 0:
                nk_ref[j] = total
            else:
                ns_ref[j * block:(j + 1) * block, :] = total
    new_ref[...] = add_small(small_ref[...], got_ref, parts * block)
    put_small(ns_ref, kept * block, new_ref[...])


def fold_small(order, keep, got, small, mine, bit, **more):
    parts, block, cols = keep.shape
    extra = got.shape[0] - parts * block
    return call(
        order, functools.partial(fold_small_kernel, bit=bit),
        [shape((parts // 2, block, cols), bf16), shape((parts // 2 * block + extra, cols), bf16),
         shape(small.shape, f32)], [mine, keep, got, small], "fold_small", 2 * keep.size, smem=1, **more)


def weight_kernel(mine_ref, *refs, groups, bit, tile):
    keep_ref, send_ref, lt_ref, acc_ref = refs[-4:]
    kept, block, cols = keep_ref.shape
    products = []
    at = 0
    for lefts, rights, first, stop in groups:
        start = 0
        for x in refs[at:at + lefts]:
            n = x.shape[0]
            lt_ref[:, start:start + n] = x[...].T
            start += n
        at += lefts
        right = [x[:, first:stop] for x in refs[at:at + rights]]
        at += rights
        right = jnp.concatenate(right, axis=0) if rights > 1 else right[0]
        if len(groups) > 1:
            products.append(mm(lt_ref[...], right))
    mine = mine_ref[0]
    for c0 in range(0, cols, tile):
        c1 = min(cols, c0 + tile)
        if products:
            acc_ref[:, :c1 - c0] = jnp.concatenate(products, axis=1)
        else:
            acc_ref[:, :c1 - c0] = mm(lt_ref[...], right[:, c0:c1])
        for j in range(kept):
            for ref, side in ((keep_ref, mine), (send_ref, 1 - mine)):
                row_at = pl.multiple_of(insert_bit(j, bit, side) * block, block)
                ref[j, :, c0:c1] = acc_ref[pl.ds(row_at, block), :c1 - c0].astype(bf16)


def weight_grad(order, groups, mine, bit, parts, name, tile=384, **more):
    width = groups[0][0][0].shape[1]
    count = sum(x.shape[0] for x in groups[0][0])
    cols = sum(stop - first for _, _, first, stop in groups)
    block = width // parts
    if len(groups) > 1:
        tile = cols
    ins = [mine]
    for lefts, rights, _, _ in groups:
        ins += list(lefts) + list(rights)
    sizes = tuple((len(lefts), len(rights), first, stop) for lefts, rights, first, stop in groups)
    return call(
        order, functools.partial(weight_kernel, groups=sizes, bit=bit, tile=tile),
        [shape((parts // 2, block, cols), bf16)] * 2, ins, name, 2 * width * count * cols,
        scratch=[pltpu.VMEM((width, count), bf16), pltpu.VMEM((width, min(tile, cols)), f32)], smem=1, **more)


def fold_kernel(mine_ref, keep_ref, got_ref, nk_ref, ns_ref, *, bit):
    mine = mine_ref[0]
    for j in range(nk_ref.shape[0]):
        for ref, side in ((nk_ref, mine), (ns_ref, 1 - mine)):
            at = insert_bit(j, bit, side)
            ref[j] = (keep_ref[at].astype(f32) + got_ref[at].astype(f32)).astype(bf16)


def fold(order, keep, got, mine, bit, **more):
    parts, block, cols = keep.shape
    return call(order, functools.partial(fold_kernel, bit=bit), [shape((parts // 2, block, cols), bf16)] * 2,
                [mine, keep, got], "fold", 2 * keep.size, smem=1, **more)


def tick_kernel():
    pass


def tick(order, waits):
    call(order, tick_kernel, [], [], "tick", 2e11, waits=waits)


def join_kernel(a, b, out):
    out[...] = (a[...] + b[...].astype(f32)).astype(bf16)


def join(order, a, b, **more):
    return call(order, join_kernel, [shape(a.shape, bf16)], [a, b], "join", a.size, **more)[0]


def finish_kernel(keep_ref, got_ref, out_ref):
    out_ref[...] = keep_ref[0].astype(f32) + got_ref[0].astype(f32)


def finish(order, keep, got, **more):
    return call(order, finish_kernel, [shape(keep.shape[1:], f32)], [keep, got], "finish", keep.size, **more)[0]


def split_kernel(ka, ga, small, kb, gb, qkv_ref, out_ref, new_ref):
    block = ka.shape[1]
    new_ref[...] = add_small(small[...], ga, block)
    whole = jnp.concatenate(
        [ka[0].astype(f32) + ga[:block, :].astype(f32), kb[0].astype(f32) + gb[0].astype(f32)], axis=1)
    cols = out_ref.shape[1]
    for i in range(3):
        qkv_ref[i] = whole[:, i * cols:(i + 1) * cols]
    out_ref[...] = whole[:, 3 * cols:]


def finish_split(order, ka, ga, small, kb, gb, cols, **more):
    rows = ka.shape[1]
    return call(
        order, split_kernel,
        [shape((3, rows, cols), f32), shape((rows, cols), f32), shape(small.shape, f32)],
        [ka, ga, small, kb, gb], "finish_split", ka.size, **more)


def mid_kernel(res, cot, vec, g0, r1, ry, w0, w1, w2, w3, gr_ref, gb_ref, a0, a1, a2, a3, sum_ref):
    unit, inverse = unit_of(res[...])
    top = cot[...].astype(f32)
    grad = g0[...] + r1[...].astype(f32) + ry[...].astype(f32)
    resid = top + norm_back(grad, unit, inverse, vec[GAIN2:GAIN2 + 1, :])
    gr_ref[...] = resid
    leave(gr_ref)
    branch = resid.astype(bf16)
    gb_ref[...] = branch
    for i, x in enumerate((resid, grad * unit, grad, top)):
        sum_ref[i:i + 1, :] = jnp.sum(x, axis=0, keepdims=True)
    leave(sum_ref)
    for a, w in ((a2, w2), (a3, w3), (a1, w1), (a0, w0)):
        a[...] = mm(branch, w[...], NT).astype(bf16)


def mid(order, res, cot, vec, g0, r1, ry, ws, **more):
    rows, width = g0.shape
    cols = ws[0].shape[0]
    return call(
        order, mid_kernel,
        [Far(shape((rows, width), f32)), shape((rows, width), bf16)] + [shape((rows, cols), bf16)] * 4
        + [Far(shape((4, width), f32))],
        [Far(res), Far(cot), Far(vec), Far(g0), r1, ry] + list(ws), "mid", 2 * rows * width * width, **more)


def grad_norm_kernel(g, w, xa, xb, keep_ref, send_ref, sum_ref):
    rows = xa.shape[0]
    sums = [0.0, 0.0]
    for i, (x, ref) in enumerate(((xa, keep_ref), (xb, send_ref))):
        r = slice(i * rows, (i + 1) * rows)
        grad = mm(g[r], w[...])
        ref[...] = grad.astype(ref.dtype)
        leave(ref)
        unit, _ = unit_of(x[...].astype(f32))
        sums[0] = sums[0] + jnp.sum(grad * unit, axis=0, keepdims=True)
        sums[1] = sums[1] + jnp.sum(grad, axis=0, keepdims=True)
    sum_ref[0:1, :] = sums[0]
    sum_ref[1:2, :] = sums[1]


def grad_norm(order, g, w, xa, xb, far_keep, **more):
    rows, width = xa.shape
    keep = shape((rows, width), f32)
    return call(
        order, grad_norm_kernel,
        [Far(keep) if far_keep else keep, shape((rows, width), bf16), Far(shape((2, width), f32))],
        [g, w, Far(xa), Far(xb)], "grad_norm", 4 * rows * width * g.shape[1], **more)


def last_kernel(x, gr, vec, g0, r1, ry, out):
    unit, inverse = unit_of(x[...].astype(f32))
    grad = g0[...] + r1[...].astype(f32) + ry[...].astype(f32)
    out[...] = (gr[...] + norm_back(grad, unit, inverse, vec[GAIN1:GAIN1 + 1, :])).astype(bf16)


def last(order, x, gr, vec, g0, r1, ry, **more):
    return call(order, last_kernel, [Far(shape(x.shape, bf16))], [Far(x), Far(gr), Far(vec), Far(g0), r1, ry], "last",
                20 * x.size, **more)[0]


def make_local(dp_size, tensor_size):
    def scatter_plain(groups):
        index = lax.axis_index("dp")
        value = jnp.concatenate(
            [mm(jnp.concatenate(lefts), jnp.concatenate([x[:, first:stop] for x in rights]), TN)
             for lefts, rights, first, stop in groups], axis=1).astype(bf16)
        width, cols = value.shape
        block = width // dp_size
        bit = 1
        while bit < dp_size:
            count = value.shape[0] // block // 2
            pairs = value.reshape(count, 2, block, cols)
            mine = (index // bit) % 2
            keep = lax.dynamic_index_in_dim(pairs, mine, 1, keepdims=False)
            send = lax.dynamic_index_in_dim(pairs, 1 - mine, 1, keepdims=False)
            value = keep.astype(f32) + swap(send, "dp", dp_size, bit).astype(f32)
            bit *= 2
            if bit < dp_size:
                value = value.astype(bf16)
            value = value.reshape(count * block, cols)
        return value

    class Spread:
        def __init__(self, order, groups, bits, name, **more):
            width = groups[0][0][0].shape[1]
            self.order, self.bits, self.index = order, bits, lax.axis_index("dp")
            self.paired = dp_size == 8 and (width // dp_size) % 16 == 0
            if self.paired:
                self.step = 0
                self.keep, send = weight_grad(order, groups, self.mine(bits[0]), bits[0], dp_size, name, **more)
                self.got = swap(after(send, order.last), "dp", dp_size, bits[0])
            else:
                self.value = scatter_plain(groups)

        def mine(self, bit):
            return ((self.index // bit) % 2).astype(jnp.int32).reshape(1)

        def local_bit(self):
            bit = local = self.bits[self.step]
            for used in self.bits[:self.step]:
                if used < bit:
                    local //= 2
            return bit, local

        def fold(self, **more):
            if self.paired:
                self.step += 1
                bit, local_bit = self.local_bit()
                self.keep, send = fold(self.order, self.keep, self.got, self.mine(bit), local_bit, **more)
                self.got = swap(after(send, self.order.last), "dp", dp_size, bit)

        def result(self, **more):
            if self.paired:
                return finish(self.order, self.keep, self.got, **more)
            return self.value

    class SpreadSmall(Spread):
        def __init__(self, order, lefts, rights, smalls, first, stop, bits, name, **more):
            width = lefts[0].shape[1]
            self.order, self.bits, self.index, self.step = order, bits, lax.axis_index("dp"), 0
            self.keep, send, self.small = weight_small(
                order, lefts, rights, smalls, first, stop, self.mine(bits[0]), bits[0], dp_size, name, **more)
            self.got = swap(after(send, order.last), "dp", dp_size, bits[0])

        def fold(self, **more):
            self.step += 1
            bit, local_bit = self.local_bit()
            self.keep, send, self.small = fold_small(
                self.order, self.keep, self.got, self.small, self.mine(bit), local_bit, **more)
            self.got = swap(after(send, self.order.last), "dp", dp_size, bit)

    def local(hidden_in, picture_ids, norm1_gain, norm1_bias, w_qkv, qv_bias, w_out, out_bias,
              norm2_gain, norm2_bias, w_up, up_bias, w_down, down_bias, cotangent):
        rows, width = hidden_in.shape
        head_width = w_qkv.shape[2]
        place = lax.axis_index("tensor")
        order = Order()
        units = w_up.shape[1]
        wt_qkv = w_qkv.transpose(0, 2, 1).reshape(3 * head_width, width)
        wt_up = w_up.T
        index = lax.axis_index("dp")

        def pin(value):
            return value if order.last is None else after(value, order.last)

        def core(value):
            return swap(pin(value), "tensor", tensor_size, 1)

        def across(value):
            return swap(pin(value), "tensor", tensor_size, 2)

        def diagonal(value):
            return swap(pin(value), "tensor", tensor_size, 3)

        def double(value, bit):
            other = swap(pin(value), "dp", dp_size, bit)
            low = (index // bit) % 2 == 0
            return jnp.concatenate([jnp.where(low, value, other), jnp.where(low, other, value)])

        paired = dp_size == 8 and (width // dp_size) % 16 == 0
        h2 = across(hidden_in)
        h1, c1, w1 = core(hidden_in), core(cotangent), core(w_out)
        mark_q, mark_k, vec = marks(
            order, place.astype(jnp.int32).reshape(1), picture_ids.reshape(tensor_size, rows),
            [norm1_gain, norm1_bias, norm2_gain, norm2_bias, out_bias, up_bias, qv_bias, down_bias])
        nn, pn, pn_far = qkv(order, hidden_in, h1, vec, wt_qkv)
        h3 = core(h2)
        w2 = across(after(w_out, h2))
        nf, pf, pf_far = qkv(order, h2, h3, vec, wt_qkv, waits=[c1])
        a2, a3, lse_f, top_f = attend(order, pf, pn, pf, mark_q, mark_k, 2 * rows, waits=[w1])
        got2, got3 = across(a2), diagonal(a3)
        a0, a1, lse_n, top_n = attend(order, pn, pn, pf, mark_q, mark_k, 0)
        got1, w3 = core(a1), core(w2)
        c2 = across(cotangent)
        ga_n = grad_act_of(order, cotangent, c1, w_down)
        tick(order, [got2, got3])
        ws = [w_out, w1, w2, w3]
        residual, normed_b = out_project(order, hidden_in, vec, [a0, got1, got2, got3], ws)
        b2, b1 = across(normed_b), core(normed_b)
        c3 = core(c2)
        act_n, pre_n, g0, g1, up_n = hidden(order, normed_b, b1, ga_n, wt_up, vec, True)
        b3, r1 = core(b2), core(g1)
        ga_f = grad_act_of(order, c2, c3, w_down)
        act_f, pre_f, g2, g3, up_f = hidden(order, b2, b3, ga_f, wt_up, vec, False)
        r3 = core(g3)
        m0, m1 = down(order, act_n, w_down, True, waits=[r1])
        n1 = core(m1)
        ry = across(join(order, g2, r3))
        s_up = Spread(order, [([normed_b, b1, b2, b3], [pre_n, pre_f], 0, units)], (1, 2, 4), "weight_up")
        s_down = Spread(order, [([cotangent, c1, c2, c3], [act_n, act_f], 0, units)], (1, 2, 4), "weight_down",
                        waits=[n1])
        grad_resid, branch, p0, p1, p2, p3, sums_b = mid(order, residual, cotangent, vec, g0, r1, ry, ws)
        d = [p0, core(p1), across(p2), diagonal(p3)]
        m2, m3 = down(order, act_f, w_down, False)
        n3 = core(m3)
        s_up.fold()
        n2 = join(order, m2, n3)
        gb2 = across(after(branch, d[2], d[3]))
        gq_n, gq_f, sums_qv = attend_back(
            order, pn_far, pf_far, d, [a0, a1, a2, a3], lse_n, lse_f, mark_q, mark_k)
        gb3, gb1 = core(gb2), core(branch)
        s_up.fold()
        e2, e3, sums_f = grad_norm(order, gq_f, wt_qkv, h2, h3, False)
        f3 = core(e3)
        cut = 512 if paired else head_width
        s_down.fold()
        s_vo = Spread(order, [([nn, nf], [gq_n, gq_f], cut, 3 * head_width),
                              ([branch, gb1, gb2, gb3], [a0, a1, a2, a3], 0, head_width)], (1, 2, 4), "weight_vo")
        fy = across(join(order, e2, f3))
        e0, e1, sums_n = grad_norm(order, gq_n, wt_qkv, hidden_in, h1, True)
        f1 = core(e1)
        smalls = [sums_n, sums_f, sums_b, up_n, up_f, sums_qv, top_n, top_f]
        if paired:
            s_qk = SpreadSmall(order, [nn, nf], [gq_n, gq_f], smalls, 0, cut, (2, 1, 4), "weight_qk")
        else:
            s_qk = Spread(order, [([nn, nf], [gq_n, gq_f], 0, cut)], (2, 1, 4), "weight_qk")
        g_up = s_up.result()
        s_down.fold()
        ny = across(after(n2, fy))
        s_vo.fold()
        grad_in = last(order, hidden_in, grad_resid, vec, e0, f1, fy)
        s_qk.fold()
        s_vo.fold()
        g_down = s_down.result()
        s_qk.fold()
        hidden_out = (residual + m0 + n1.astype(f32) + ny.astype(f32) + down_bias).astype(bf16)
        if paired:
            g_qkv, g_out, small = finish_split(order, s_qk.keep, s_qk.got, s_qk.small, s_vo.keep, s_vo.got, head_width,
                                               waits=[hidden_out])
        else:
            last_w = jnp.concatenate([s_qk.result(), s_vo.result()], axis=1)
            g_qkv = jnp.stack([last_w[:, i * head_width:(i + 1) * head_width] for i in range(3)])
            g_out = last_w[:, 3 * head_width:]
            wide = lambda x: jnp.pad(x, ((0, 0), (0, width - x.shape[1])))
            small = jnp.concatenate([sums_n + sums_f, sums_b, wide(up_n + up_f), wide(sums_qv),
                                     wide(jnp.maximum(top_n, top_f))])
            bit = 1
            while bit < dp_size:
                other = swap(small, "dp", dp_size, bit)
                small = jnp.concatenate([small[:TOP_ROW] + other[:TOP_ROW], jnp.maximum(small[TOP_ROW:], other[TOP_ROW:])])
                bit *= 2
        shared = small[:8]
        shared = shared + swap(shared, "tensor", tensor_size, 1)
        shared = shared + swap(shared, "tensor", tensor_size, 2)
        top = small[TOP_ROW, :head_width // HEAD_DIM]
        limit = jnp.float32(CLIP_LIMIT)
        factor = jnp.sqrt(limit / jnp.maximum(top, limit))
        column = jnp.repeat(factor, HEAD_DIM)
        scaled_qk = (w_qkv[:2].astype(f32) * column).astype(bf16)
        scaled_query_bias = qv_bias[0] * column
        return (hidden_out, grad_in, g_qkv, g_out.T, g_up, g_down.T, small[7:9, :head_width], small[6, :units],
                shared[:6], top, scaled_qk, scaled_query_bias)

    return local


def solution(mesh):
    return jax.shard_map(
        make_local(mesh.shape["dp"], mesh.shape["tensor"]),
        mesh=mesh,
        in_specs=(
            P(("dp", "tensor"), None), P("dp"), P(), P(), P(None, None, "tensor"), P(None, "tensor"),
            P("tensor", None), P(), P(), P(), P(None, "tensor"), P("tensor"), P("tensor", None), P(),
            P(("dp", "tensor"), None),
        ),
        out_specs=(
            P(("dp", "tensor"), None), P(("dp", "tensor"), None), P(None, "dp", "tensor"), P("tensor", "dp"),
            P("dp", "tensor"), P("tensor", "dp"), P(None, "tensor"), P("tensor"), P(), P("tensor"),
            P(None, None, "tensor"), P("tensor"),
        ),
        check_vma=False,
    )
```
